128 devices in a mesh: ep: 16 (over x, z), sp: 8 (over y, core).
Axes of the slice: x: 4, y: 4, z: 4, core: 2. Of those that a mesh axis runs over, the one named last changes fastest.
Arguments:
- tokens: bfloat16 [16384, 3584], P(('ep', 'sp')), may hold values from -40 to 40
- cotangent: bfloat16 [16384, 3584], P(('ep', 'sp')), may hold values from -11 to 11
- norm_gain: float32 [3584], replicated, may hold values from 0.1 to 1.9
- router: float32 [3584, 16], replicated, may hold values from -0.09375 to 0.09375
- dense_gate: bfloat16 [3584, 2432], P(None, 'sp'), may hold values from -0.09375 to 0.09375
- dense_up: bfloat16 [3584, 2432], P(None, 'sp'), may hold values from -0.09375 to 0.09375
- dense_down: bfloat16 [2432, 3584], P('sp'), may hold values from -0.125 to 0.125
- expert_gate: bfloat16 [16, 3584, 2432], P('ep', None, 'sp'), may hold values from -0.09375 to 0.09375
- expert_up: bfloat16 [16, 3584, 2432], P('ep', None, 'sp'), may hold values from -0.09375 to 0.09375
- expert_down: bfloat16 [16, 2432, 3584], P('ep', 'sp'), may hold values from -0.125 to 0.125
- routes: int32 [16384, 2], P(('ep', 'sp')), may hold values from 0 to 15, all different within a row; in each aligned block of 128 rows (0 to 127, 128 to 255, ...) at most 20 rows name the same one
Outputs:
- input_grad: bfloat16 [16384, 3584], P(('ep', 'sp'))
- gain_grad: float32 [3584], replicated
- router_grad: float32 [3584, 16], replicated
The draws below stay inside these ranges and needn't reach their ends.
Inputs may be any that keep to these rules, and one draw needn't show every extreme that they name: `routes`: each token names two different experts. Among the rows of one device no expert is named more than 20 times, and in some devices one expert is named exactly 20 times.
All inputs are finite; a program needn't handle non-finite values.
Results may differ from the reference program's by a relative error of at most 0.013.
Values may be sent and summed in bfloat16 or wider, within the bound.
No kernel may reach another device: no remote copies, remote signals or barrier semaphores. Data moves between devices by JAX's collectives and lax.ppermute only.
A program may use at most 256 MiB of HBM per device.

```python
import math
import jax
import jax.numpy as jnp
import numpy as np
from jax import lax

D = 3584
FF = 2432
FE = 2432
TOK_DEV = 128
EXPERTS = 16
CAP = 20
TOKENS = 16384
N_EP = 16
N_SP = 8


def draw_tokens(key, part):
    key = jax.random.fold_in(key, 11)
    key_base, key_rows, key_cols = jax.random.split(key, 3)
    rows = 10.0 ** jax.random.uniform(key_rows, (TOKENS, 1), jnp.float32)
    cols = 10.0 ** jax.random.uniform(key_cols, (1, D), jnp.float32)
    base = jnp.clip(jax.random.normal(key_base, (TOKENS, D), jnp.float32), -4.0, 4.0)
    return (0.1 * base * rows * cols).astype(jnp.bfloat16)


def draw_cotangent(key, part):
    key = jax.random.fold_in(key, 23)
    key_base, key_rows = jax.random.split(key, 2)
    rise = 3.0 ** (jnp.arange(TOKENS, dtype=jnp.float32) / (TOKENS - 1))
    rows = 3.0 ** jax.random.uniform(key_rows, (TOKENS, 1), jnp.float32)
    base = jnp.clip(jax.random.normal(key_base, (TOKENS, D), jnp.float32), -4.0, 4.0)
    return (0.3 * base * rise[:, None] * rows).astype(jnp.bfloat16)


def block_levels(key, shape, cuts, smallest, top_value):
    level = 1.0
    for dim, parts in cuts:
        heights = jax.random.uniform(jax.random.fold_in(jax.random.fold_in(key, 6), dim), (parts,), jnp.float32, smallest / len(cuts), top_value / len(cuts))
        level = level * jnp.repeat(jnp.exp(heights), shape[dim] // parts).reshape((-1,) + (1,) * (len(shape) - 1 - dim))
    return level


def deal_out(key, own, number, rows, count, top, reach, slope):
    order = jax.random.permutation(key, count)
    heavy_load, usual = shares(count, rows * top, reach, slope, True), shares(count, rows * top, reach, slope, False)
    places = jnp.arange(count)

    def named(sizes, offset_by):
        used = int((sizes > 0).sum())
        fixed = max(1, used // 4)
        moved = fixed + (places - fixed + offset_by * (used - fixed)) % max(1, count - fixed)
        return jnp.zeros((count,), jnp.int32).at[order[jnp.where(places < fixed, places, moved)]].set(jnp.asarray(sizes, jnp.int32))

    sizes = jnp.where(number % 4 == 0, named(heavy_load, number // 4), named(usual, number - number // 4 - 1))
    mixed = jax.random.permutation(jax.random.fold_in(own, 3), count)
    source_of, sink = mixed[0:count // 2 * 2:2], mixed[1:count // 2 * 2:2]
    slack = jnp.minimum(sizes[source_of] - 1, reach - sizes[sink]) // 2
    slack = jnp.where((source_of == order[0]) | (sink == order[0]) | (sizes[sink] == 0), 0, jnp.maximum(slack, 0))
    moved = jax.random.randint(jax.random.fold_in(own, 4), (count // 2,), 0, 1 << 20) % (slack + 1)
    sizes = sizes.at[source_of].add(-moved).at[sink].add(moved)
    members = jnp.searchsorted(jnp.cumsum(sizes), jnp.arange(rows * top), side="right").astype(jnp.int32)
    listing = members.reshape(top, rows).T
    listing = listing[jax.random.permutation(jax.random.fold_in(own, 1), rows)]
    offset_by = jax.random.randint(jax.random.fold_in(own, 2), (rows, 1), 0, top)
    return jnp.take_along_axis(listing, (jnp.arange(top)[None, :] + offset_by) % top, axis=1)


def shares(count, total, limit, slope, full):
    loads = [(1 << 20) // math.isqrt(standing ** slope) + 1 for standing in range(1, count + 1)]
    largest = limit if full else min(limit, max(-(-total // count), total * loads[0] // sum(loads)))
    least = 1 if total - largest >= count - 1 else 0
    given, surplus = [largest] + [least] * (count - 1), total - largest - least * (count - 1)
    while surplus > 0:
        movable = [i for i in range(1, count) if given[i] < largest] or [i for i in range(1, count) if given[i] < limit]
        whole, budget = sum([loads[i] for i in movable]), surplus
        for i in movable:
            extra = min(limit - given[i], max(1, budget * loads[i] // whole), surplus)
            given[i] = given[i] + extra
            surplus = surplus - extra
    return np.array(given)


def scatter_about(stream_key, shape, spread, reach, shards=(), kind=jnp.bfloat16):
    array = jax.random.normal(stream_key, shape, jnp.float32) * spread
    if len(shards) > 0:
        array = block_levels(stream_key, shape, shards, -0.22, 0.18) * array
    return jnp.clip(array, min=-reach, max=reach).astype(kind)


def setup_inputs(seed: int = 0) -> dict:
    streams_of = jax.random.split(jax.random.key(seed), 12)
    tokens = draw_tokens(jax.random.fold_in(streams_of[11], 71), 0)
    cotangent = draw_cotangent(jax.random.fold_in(streams_of[11], 71), 0)
    norm_gain = jnp.clip(1.0 + 0.18 * jax.random.normal(streams_of[2], (D,), jnp.float32), 0.1, 1.9)
    router = scatter_about(streams_of[3], (D, EXPERTS), D ** -0.5, 0.09375, (), jnp.float32)
    dense_gate = scatter_about(streams_of[4], (D, FF), D ** -0.5, 0.09375, ((1, 8),))
    dense_up = scatter_about(streams_of[5], (D, FF), D ** -0.5, 0.09375, ((1, 8),))
    dense_down = scatter_about(streams_of[6], (FF, D), FF ** -0.5, 0.125, ((0, 8),))
    expert_gate = scatter_about(streams_of[7], (EXPERTS, D, FE), D ** -0.5, 0.09375, ((0, 16), (2, 8)))
    expert_up = scatter_about(streams_of[8], (EXPERTS, D, FE), D ** -0.5, 0.09375, ((0, 16), (2, 8)))
    expert_down = scatter_about(streams_of[9], (EXPERTS, FE, D), FE ** -0.5, 0.125, ((0, 16), (1, 8)))
    routes_keys = jax.random.split(jax.random.fold_in(streams_of[10], 1), TOKENS // TOK_DEV)
    routes_turns = jax.random.permutation(jax.random.fold_in(streams_of[10], 3), TOKENS // TOK_DEV)
    routes = jax.vmap(lambda own, number: deal_out(jax.random.fold_in(streams_of[10], 2), own, number, TOK_DEV, EXPERTS, 2, CAP, 2))(routes_keys, routes_turns).reshape((TOKENS, 2))
    return dict(tokens=tokens, cotangent=cotangent, norm_gain=norm_gain, router=router, dense_gate=dense_gate, dense_up=dense_up, dense_down=dense_down, expert_gate=expert_gate, expert_up=expert_up, expert_down=expert_down, routes=routes)


EPS = 1e-05

def silu_slope(gate):
    sig = jax.nn.sigmoid(gate)
    return sig * (1.0 + gate * (1.0 - sig))

def hidden_grads(rows_n, rows_dy, w_gate, w_up, w_down):
    gate = jnp.dot(rows_n, w_gate, preferred_element_type=jnp.float32)
    up = jnp.dot(rows_n, w_up, preferred_element_type=jnp.float32)
    back = lax.dot_general(rows_dy, w_down, (((1,), (1,)), ((), ())), preferred_element_type=jnp.float32)
    active = jax.nn.silu(gate)
    grad_up = (back * active).astype(jnp.bfloat16)
    grad_gate = (back * up * silu_slope(gate)).astype(jnp.bfloat16)
    into = lax.dot_general(grad_gate, w_gate, (((1,), (1,)), ((), ())), preferred_element_type=jnp.float32)
    into = into + lax.dot_general(grad_up, w_up, (((1,), (1,)), ((), ())), preferred_element_type=jnp.float32)
    return (into.astype(jnp.bfloat16), lax.optimization_barrier(jnp.sum(active * up * back, -1)).astype(jnp.bfloat16))

def lift(value):
    return lax.optimization_barrier(value).astype(jnp.float32)

def reference(tokens, cotangent, norm_gain, router, dense_gate, dense_up, dense_down, expert_gate, expert_up, expert_down, routes):
    values = tokens.astype(jnp.float32)
    inverse = lax.rsqrt(lax.optimization_barrier(jnp.mean(values * values, -1, keepdims=True)) + EPS)
    normed = (values * inverse * norm_gain).astype(jnp.bfloat16)
    hi = lax.Precision.HIGHEST
    dense_block = FF // N_SP
    dense_into = jnp.zeros((TOKENS, D), jnp.float32)
    for shard in range(N_SP):
        low = shard * dense_block
        part, unused = hidden_grads(normed, cotangent, dense_gate[:, low:low + dense_block], dense_up[:, low:low + dense_block], dense_down[low:low + dense_block, :])
        dense_into = dense_into + lift(part)
    choice_ids = jnp.arange(EXPERTS, dtype=jnp.int32)
    first = (routes[:, 0:1] == choice_ids[None, :]).astype(jnp.float32)
    second = (routes[:, 1:2] == choice_ids[None, :]).astype(jnp.float32)
    logits = jnp.dot(normed.astype(jnp.float32), router, precision=hi)
    weight_one = jax.nn.sigmoid(lax.optimization_barrier(jnp.sum(logits * first, -1)) - lax.optimization_barrier(jnp.sum(logits * second, -1)))
    weight_two = 1.0 - weight_one
    slots_all = N_EP * N_SP * CAP
    flat_ids = routes.reshape(-1)
    hits = (flat_ids[:, None] == choice_ids[None, :]).astype(jnp.int32)
    places = jnp.cumsum(hits, 0) - hits
    slot = lax.optimization_barrier(jnp.sum(hits * places, 1)).astype(jnp.int32)
    owners = (jnp.arange(2 * TOKENS, dtype=jnp.int32) // 2).astype(jnp.int32)
    table = jnp.full((EXPERTS, slots_all), TOKENS, jnp.int32).at[flat_ids, slot].set(owners)
    padded_n = jnp.concatenate([normed, jnp.zeros((1, D), jnp.bfloat16)], 0)
    padded_dy = jnp.concatenate([cotangent, jnp.zeros((1, D), jnp.bfloat16)], 0)
    expert_block = FE // N_SP

    def one_expert(inputs):
        index, w_gate, w_up, w_down = inputs
        rows_n = padded_n[index]
        rows_dy = padded_dy[index]
        into = jnp.zeros((slots_all, D), jnp.float32)
        score = jnp.zeros((slots_all,), jnp.float32)
        for shard in range(N_SP):
            low = shard * expert_block
            part, joint = hidden_grads(rows_n, rows_dy, w_gate[:, low:low + expert_block], w_up[:, low:low + expert_block], w_down[low:low + expert_block, :])
            into = into + lift(part)
            score = score + lift(joint)
        return (into, score)
    expert_into, expert_score = lax.map(one_expert, (table, expert_gate, expert_up, expert_down))
    slot_pair = slot.reshape(TOKENS, 2)
    into_one = expert_into[routes[:, 0], slot_pair[:, 0]]
    into_two = expert_into[routes[:, 1], slot_pair[:, 1]]
    score_one = expert_score[routes[:, 0], slot_pair[:, 0]]
    score_two = expert_score[routes[:, 1], slot_pair[:, 1]]
    delta = weight_one * weight_two * (score_one - score_two)
    grad_logits = first * delta[:, None] - second * delta[:, None]
    router_grad = jnp.dot(normed.astype(jnp.float32).T, grad_logits, precision=hi)
    total = dense_into + weight_one[:, None] * into_one + weight_two[:, None] * into_two
    total = total + jnp.dot(grad_logits, router.T, precision=hi)
    gain_grad = lax.optimization_barrier(jnp.sum(total * values * inverse, 0))
    scaled = total * norm_gain
    mean_term = lax.optimization_barrier(jnp.mean(scaled * values, -1, keepdims=True))
    input_grad = cotangent.astype(jnp.float32) + inverse * (scaled - values * inverse * inverse * mean_term)
    return (input_grad.astype(jnp.bfloat16), gain_grad, router_grad)
```

```python
import jax
import jax.numpy as jnp
from jax import lax
from jax.sharding import Mesh, PartitionSpec as P

EPS = 1e-05
BF = jnp.bfloat16
F32 = jnp.float32
HIGHEST = lax.Precision.HIGHEST
PEERS = 4
NEAR = 16


def receive_from(value, k):
    return lax.ppermute(value, "y", [(i, (i - k) % PEERS) for i in range(PEERS)])


def send_to(value, k):
    return lax.ppermute(value, "y", [(i, (i + k) % PEERS) for i in range(PEERS)])


def swap(value):
    return lax.ppermute(value, "core", [(0, 1), (1, 0)])


def over_ep(value):
    return lax.all_to_all(value, "ep", split_axis=0, concat_axis=0, tiled=True)


def join_weights(gate, up, down):
    hidden = 2 * gate.shape[1]
    pad = -hidden % 128
    blank = jnp.zeros((gate.shape[0], pad), BF)
    wide = jnp.concatenate([gate, swap(gate), blank, up, swap(up), blank], 1)
    tall = jnp.concatenate([down, swap(down), jnp.zeros((pad, down.shape[1]), BF)], 0)
    return wide, tall


def hidden_grads(rows, wide, tall):
    width = tall.shape[1]
    half = tall.shape[0]
    both = jnp.dot(rows[:, :width], wide, preferred_element_type=F32)
    back = lax.dot_general(
        rows[:, width:], tall, (((1,), (1,)), ((), ())), preferred_element_type=F32
    )
    gate, up = both[:, :half], both[:, half:]
    sig = jax.nn.sigmoid(gate)
    active = gate * sig
    grad_up = back * active
    grad_gate = back * up * (sig * (1.0 + gate * (1.0 - sig)))
    joint = jnp.sum(grad_up * up, -1)
    grads = jnp.concatenate([grad_gate.astype(BF), grad_up.astype(BF)], 1)
    into = lax.dot_general(grads, wide, (((1,), (1,)), ((), ())), preferred_element_type=F32)
    return into, joint


def one_hot_rows(index, count):
    return index[..., None] == lax.broadcasted_iota(jnp.int32, (1, 1, count), 2)


def body(
    tokens,
    cotangent,
    norm_gain,
    router,
    dense_gate,
    dense_up,
    dense_down,
    expert_gate,
    expert_up,
    expert_down,
    routes,
):
    tok, width = tokens.shape
    experts = router.shape[1]
    cap = 5 * tok // (2 * experts)
    own_rows = -(-cap // 8) * 8
    far = cap - NEAR
    far_rows = -(-(cap + 2 * far) // 8) * 8

    values = tokens.astype(F32)
    inverse = lax.rsqrt(jnp.mean(values * values, -1, keepdims=True) + EPS)
    normed = (values * inverse * norm_gain).astype(BF)
    pair = jnp.concatenate([normed, cotangent], 1)

    all_routes = jnp.stack([routes] + [receive_from(routes, k) for k in (1, 2, 3)])
    choice_ids = lax.broadcasted_iota(jnp.int32, (1, 1, 1, experts), 3)
    chosen = all_routes[..., None] == choice_ids
    hits = chosen.reshape(PEERS, 2 * tok, experts).astype(BF)
    place = lax.broadcasted_iota(jnp.int32, (2 * tok, 2 * tok), 0)
    before = (lax.broadcasted_iota(jnp.int32, (2 * tok, 2 * tok), 1) < place).astype(BF)
    places = jnp.einsum("ab,kbe->kae", before, hits, preferred_element_type=F32)
    slots = jnp.sum(hits.astype(F32) * places, -1).astype(jnp.int32).reshape(PEERS, tok, 2)

    own_hot = one_hot_rows(all_routes[0] * own_rows + slots[0], experts * own_rows)
    own_pick = jnp.sum(own_hot.astype(BF), 1)
    own_send = lax.dot_general(
        own_pick, pair, (((0,), (0,)), ((), ())), preferred_element_type=F32
    ).astype(BF)
    own = over_ep(own_send)

    peers = [receive_from(pair, k) for k in (1, 2, 3)]
    rows_of_all = jnp.concatenate([pair] + peers, 0)

    base1 = jnp.where(slots[1] >= NEAR, slots[1] - NEAR, -4 * experts * far_rows)
    base2 = slots[2] + far
    base3 = jnp.where(slots[3] >= NEAR, slots[3] - NEAR + far + cap, -4 * experts * far_rows)
    far_index = jnp.concatenate(
        [all_routes[k] * far_rows + b for k, b in ((1, base1), (2, base2), (3, base3))], 0
    )
    far_hot = one_hot_rows(far_index, experts * far_rows)
    far_pick = jnp.sum(far_hot.astype(BF), 1)
    far_send = lax.dot_general(
        far_pick, rows_of_all[tok:], (((0,), (0,)), ((), ())), preferred_element_type=F32
    ).astype(BF)
    far_got = over_ep(far_send)

    near_send = own.reshape(experts, own_rows, 2 * width)[:, :NEAR].reshape(-1, 2 * width)
    near1 = receive_from(near_send, 1)
    near3 = receive_from(near_send, 3)

    wide_d, tall_d = join_weights(dense_gate, dense_up, dense_down)
    wide_e, tall_e = join_weights(expert_gate[0], expert_up[0], expert_down[0])

    dense_part, unused = hidden_grads(rows_of_all, wide_d, tall_d)
    own_into, own_joint = hidden_grads(own, wide_e, tall_e)
    near1_into, near1_joint = hidden_grads(near1, wide_e, tall_e)
    near3_into, near3_joint = hidden_grads(near3, wide_e, tall_e)
    far_into, far_joint = hidden_grads(far_got, wide_e, tall_e)

    own_joint = own_joint.reshape(experts, own_rows)
    near1_joint = near1_joint.reshape(experts, NEAR)
    near3_joint = near3_joint.reshape(experts, NEAR)
    far_joint = far_joint.reshape(experts, far_rows)
    joints = jnp.concatenate(
        [
            own_joint[:, :cap],
            near1_joint,
            far_joint[:, :far],
            far_joint[:, far : far + cap],
            near3_joint,
            far_joint[:, far + cap : far + cap + far],
        ],
        1,
    )
    joints = over_ep(joints).reshape(experts, PEERS, cap)
    score = joints[:, 0]
    for k in (1, 2, 3):
        score = score + send_to(joints[:, k], k)

    far_back = over_ep(far_into.astype(BF))
    near_back = send_to(near1_into.astype(BF), 1).astype(F32)
    near_back = near_back + send_to(near3_into.astype(BF), 3).astype(F32)
    near_back = near_back.reshape(experts, NEAR, width)
    own_into = own_into.reshape(experts, own_rows, width)
    own_into = jnp.concatenate([own_into[:, :NEAR] + near_back, own_into[:, NEAR:]], 1)
    own_back = over_ep(own_into.astype(BF).reshape(-1, width))

    logits = jnp.dot(rows_of_all[:, :width].astype(F32), router, precision=HIGHEST)
    logits = logits.reshape(PEERS, tok, 1, experts)
    picked = jnp.sum(jnp.where(chosen, logits, 0.0), -1)
    weight_one = jax.nn.sigmoid(picked[..., 0] - picked[..., 1])
    weights = jnp.stack([weight_one, 1.0 - weight_one], -1)

    far_mix = jnp.sum(jnp.where(far_hot, weights[1:].reshape(-1, 2)[..., None], 0.0), 1)
    part = dense_part[tok:] + jnp.dot(far_mix.astype(BF), far_back, preferred_element_type=F32)
    part = part.astype(BF).reshape(PEERS - 1, tok, width)
    home = [send_to(part[k - 1], k) for k in (1, 2, 3)]

    own_mix = jnp.sum(jnp.where(own_hot, weights[0][..., None], 0.0), 1)
    total = dense_part[:tok] + jnp.dot(own_mix.astype(BF), own_back, preferred_element_type=F32)
    for piece in home:
        total = total + piece.astype(F32)

    score = jnp.pad(score, ((0, 0), (0, own_rows - cap))).reshape(1, 1, -1)
    scores = jnp.sum(jnp.where(own_hot, score, 0.0), -1)
    delta = weights[0, :, 0] * weights[0, :, 1] * (scores[:, 0] - scores[:, 1])
    signed = chosen[0, :, 0].astype(F32) - chosen[0, :, 1].astype(F32)
    grad_logits = signed * delta[:, None]
    local_router = lax.dot_general(
        grad_logits, normed.astype(F32), (((0,), (0,)), ((), ())), precision=HIGHEST
    )
    axes = ("ep", "y", "core")
    devices = lax.axis_size(axes)
    spread = lax.all_to_all(local_router.reshape(devices, -1), axes, 0, 0, tiled=True)
    mine = jnp.sum(spread, 0, keepdims=True)
    router_grad = lax.all_to_all(
        jnp.broadcast_to(mine, (devices, mine.shape[1])), axes, 0, 0, tiled=True
    )
    router_grad = router_grad.reshape(experts, width).T

    total = total + jnp.dot(grad_logits, router.T, precision=HIGHEST)
    local_gain = jnp.sum(total * values * inverse, 0)
    gains = lax.all_to_all(
        jnp.broadcast_to(local_gain[None], (devices, width)), axes, 0, 0, tiled=True
    )
    gain_grad = jnp.sum(gains, 0)
    scaled = total * norm_gain
    mean_term = jnp.mean(scaled * values, -1, keepdims=True)
    input_grad = cotangent.astype(F32) + inverse * (
        scaled - values * inverse * inverse * mean_term
    )
    return (input_grad.astype(BF), gain_grad, router_grad)


def solution(mesh):
    ep, sp = mesh.devices.shape
    grid = Mesh(mesh.devices.reshape(ep, sp // 2, 2), ("ep", "y", "core"))
    shared = ("y", "core")
    rows = ("ep", "y", "core")
    return jax.shard_map(
        body,
        mesh=grid,
        in_specs=(
            P(rows, None),
            P(rows, None),
            P(),
            P(),
            P(None, shared),
            P(None, shared),
            P(shared, None),
            P("ep", None, shared),
            P("ep", None, shared),
            P("ep", shared, None),
            P(rows, None),
        ),
        out_specs=(P(rows, None), P(), P()),
        check_vma=False,
    )
```

```python
import jax
import jax.numpy as jnp
from jax import lax
from jax.sharding import Mesh, PartitionSpec as P

EPS = 1e-05
BF = jnp.bfloat16
F32 = jnp.float32
HIGHEST = lax.Precision.HIGHEST
PEERS = 4


def receive_from(value, k):
    return lax.ppermute(value, "y", [(i, (i - k) % PEERS) for i in range(PEERS)])


def send_to(value, k):
    return lax.ppermute(value, "y", [(i, (i + k) % PEERS) for i in range(PEERS)])


def swap(value):
    return lax.ppermute(value, "core", [(0, 1), (1, 0)])


def over_ep(value):
    return lax.all_to_all(value, "ep", split_axis=0, concat_axis=0, tiled=True)


def join_weights(gate, up, down):
    hidden = 2 * gate.shape[1]
    pad = -hidden % 128
    blank = jnp.zeros((gate.shape[0], pad), BF)
    wide = jnp.concatenate([gate, swap(gate), blank, up, swap(up), blank], 1)
    tall = jnp.concatenate([down, swap(down), jnp.zeros((pad, down.shape[1]), BF)], 0)
    return wide, tall


def hidden_grads(rows, wide, tall):
    width = tall.shape[1]
    half = tall.shape[0]
    both = jnp.dot(rows[:, :width], wide, preferred_element_type=F32)
    back = lax.dot_general(
        rows[:, width:], tall, (((1,), (1,)), ((), ())), preferred_element_type=F32
    )
    gate, up = both[:, :half], both[:, half:]
    sig = jax.nn.sigmoid(gate)
    active = gate * sig
    grad_up = back * active
    grad_gate = back * up * (sig * (1.0 + gate * (1.0 - sig)))
    joint = jnp.sum(grad_up * up, -1)
    grads = jnp.concatenate([grad_gate.astype(BF), grad_up.astype(BF)], 1)
    into = lax.dot_general(grads, wide, (((1,), (1,)), ((), ())), preferred_element_type=F32)
    return into, joint


def after(value, *others):
    return lax.optimization_barrier((value,) + others)[0]


def over_all(value):
    value = value + swap(value)
    parts = [receive_from(value, j) for j in (1, 2, 3)]
    value = (value + parts[0]) + (parts[1] + parts[2])
    count = lax.axis_size("ep")
    side = 4
    for stride, block in ((1, side), (side, count)):
        parts = []
        for j in range(1, block // stride):
            pairs = [
                (i, i // block * block + (i % block + j * stride) % block) for i in range(count)
            ]
            parts.append(lax.ppermute(value, "ep", pairs))
        for part in parts:
            value = value + part
    return value


def slot_rows(routes, experts, rows):
    tok = routes.shape[0]
    flat = routes.reshape(2 * tok, 1)
    hits = (flat == lax.broadcasted_iota(jnp.int32, (1, experts), 1)).astype(BF)
    place = lax.broadcasted_iota(jnp.int32, (2 * tok, 2 * tok), 0)
    before = (lax.broadcasted_iota(jnp.int32, (2 * tok, 2 * tok), 1) < place).astype(BF)
    places = jnp.dot(before, hits, preferred_element_type=F32)
    slots = jnp.sum(hits.astype(F32) * places, -1).astype(jnp.int32).reshape(tok, 2)
    index = routes * rows + slots
    return index[..., None] == lax.broadcasted_iota(jnp.int32, (1, 1, experts * rows), 2)


def pick(hot, rows):
    table = jnp.sum(hot.astype(BF), 1)
    return lax.dot_general(
        table, rows, (((0,), (0,)), ((), ())), preferred_element_type=F32
    ).astype(BF)


def router_weights(normed, router, chosen):
    logits = jnp.dot(normed.astype(F32), router, precision=HIGHEST)
    picked = jnp.sum(jnp.where(chosen, logits[:, None, :], 0.0), -1)
    one = jax.nn.sigmoid(picked[:, 0:1] - picked[:, 1:2])
    return jnp.concatenate([one, 1.0 - one], 1)


def mix(hot, weights, rows):
    table = jnp.sum(jnp.where(hot, weights[..., None], 0.0), 1).astype(BF)
    return jnp.dot(table, rows, preferred_element_type=F32)


def body(
    tokens,
    cotangent,
    norm_gain,
    router,
    dense_gate,
    dense_up,
    dense_down,
    expert_gate,
    expert_up,
    expert_down,
    routes,
):
    tok, width = tokens.shape
    experts = router.shape[1]
    cap = 5 * tok // (2 * experts)
    cap = -(-cap // 8) * 8

    values = tokens.astype(F32)
    inverse = lax.rsqrt(jnp.mean(values * values, -1, keepdims=True) + EPS)
    normed = (values * inverse * norm_gain).astype(BF)
    pair = jnp.concatenate([normed, cotangent], 1)

    peer2 = receive_from(pair, 2)
    routes2 = receive_from(routes, 2)
    hot = slot_rows(routes, experts, cap)
    own = over_ep(pick(hot, pair))
    later = after(pair, peer2)
    peer1 = receive_from(later, 1)
    peer3 = receive_from(later, 3)

    hot2 = slot_rows(routes2, experts, cap)
    far_send = pick(hot2, peer2)
    far = over_ep(far_send)
    near1 = receive_from(own, 1)
    near3 = receive_from(own, 3)

    wide_e, tall_e = join_weights(expert_gate[0], expert_up[0], expert_down[0])
    wide_d, tall_d = join_weights(dense_gate, dense_up, dense_down)

    own_into, own_joint = hidden_grads(after(own, far_send), wide_e, tall_e)
    dense_rows = jnp.concatenate([pair, peer1, peer2, peer3], 0)
    dense_part, unused = hidden_grads(after(dense_rows, own_into), wide_d, tall_d)
    home1 = send_to(dense_part[tok : 2 * tok].astype(BF), 1)
    home3 = send_to(dense_part[3 * tok :].astype(BF), 3)

    far_into, far_joint = hidden_grads(after(far, dense_part), wide_e, tall_e)
    far_into = far_into.astype(BF)
    far_back = over_ep(far_into)
    near1_into, near1_joint = hidden_grads(after(near1, far_into), wide_e, tall_e)
    near1_back = send_to(near1_into.astype(BF), 1)
    near3_into, near3_joint = hidden_grads(after(near3, near1_into), wide_e, tall_e)
    near3_back = send_to(near3_into.astype(BF), 3)

    joints = jnp.stack([own_joint, near1_joint, far_joint, near3_joint])
    joints = joints.reshape(4, experts, cap).transpose(1, 0, 2).reshape(experts, 4 * cap)
    joints = over_ep(after(joints, far_back))
    own_into = own_into + near1_back.astype(F32) + near3_back.astype(F32)
    own_back = over_ep(after(own_into.astype(BF), joints))

    ids = lax.broadcasted_iota(jnp.int32, (1, 1, experts), 2)
    chosen = routes[..., None] == ids
    weights = router_weights(normed, router, chosen)
    weights2 = router_weights(peer2[:, :width], router, routes2[..., None] == ids)

    part = dense_part[2 * tok : 3 * tok] + mix(hot2, weights2, far_back)
    home2 = send_to(part.astype(BF), 2)

    joints = joints.reshape(experts, 4, cap)
    score = joints[:, 0]
    for k in (1, 2, 3):
        score = score + send_to(joints[:, k], k)
    scores = jnp.sum(jnp.where(hot, score.reshape(1, 1, -1), 0.0), -1)
    delta = weights[:, 0] * weights[:, 1] * (scores[:, 0] - scores[:, 1])
    signed = chosen[:, 0].astype(F32) - chosen[:, 1].astype(F32)
    grad_logits = signed * delta[:, None]
    local_router = lax.dot_general(
        grad_logits, normed.astype(F32), (((0,), (0,)), ((), ())), precision=HIGHEST
    )
    router_grad = over_all(local_router).T
    early = dense_part[:tok] + jnp.dot(grad_logits, router.T, precision=HIGHEST)

    total = early + mix(hot, weights, own_back)
    for piece in (home1, home3, home2):
        total = total + piece.astype(F32)
    local_gain = jnp.sum(total * values * inverse, 0)
    axes = ("ep", "y", "core")
    devices = lax.axis_size(axes)
    gains = lax.all_to_all(
        jnp.broadcast_to(local_gain[None], (devices, width)), axes, 0, 0, tiled=True
    )
    gain_grad = jnp.sum(gains, 0)
    scaled = total * norm_gain
    mean_term = jnp.mean(scaled * values, -1, keepdims=True)
    input_grad = cotangent.astype(F32) + inverse * (
        scaled - values * inverse * inverse * mean_term
    )
    return (input_grad.astype(BF), gain_grad, router_grad)


def solution(mesh):
    ep, sp = mesh.devices.shape
    grid = Mesh(mesh.devices.reshape(ep, sp // 2, 2), ("ep", "y", "core"))
    shared = ("y", "core")
    rows = ("ep", "y", "core")
    return jax.shard_map(
        body,
        mesh=grid,
        in_specs=(
            P(rows, None),
            P(rows, None),
            P(),
            P(),
            P(None, shared),
            P(None, shared),
            P(shared, None),
            P("ep", None, shared),
            P("ep", None, shared),
            P("ep", shared, None),
            P(rows, None),
        ),
        out_specs=(P(rows, None), P(), P()),
        check_vma=False,
    )
```

```python
import jax
import jax.numpy as jnp
from jax import lax
from jax.experimental import pallas as pl
from jax.experimental.pallas import tpu as pltpu
from jax.sharding import Mesh, PartitionSpec as P

EPS = 1e-05
BF = jnp.bfloat16
F32 = jnp.float32
HIGHEST = lax.Precision.HIGHEST
PEERS = 4
NEAR = 16
VMEM_LIMIT = 44 * 1024 * 1024


def receive_from(value, k):
    return lax.ppermute(value, "y", [(i, (i - k) % PEERS) for i in range(PEERS)])


def send_to(value, k):
    return lax.ppermute(value, "y", [(i, (i + k) % PEERS) for i in range(PEERS)])


def swap(value):
    return lax.ppermute(value, "core", [(0, 1), (1, 0)])


def over(value, axes="ep"):
    return lax.all_to_all(value, axes, split_axis=0, concat_axis=0, tiled=True)


def after(value, *others):
    return lax.optimization_barrier((value,) + others)[0]


def join_weights(gate, up, down):
    hidden = 2 * gate.shape[1]
    pad = -hidden % 128
    blank = jnp.zeros((gate.shape[0], pad), BF)
    wide = jnp.concatenate([gate, swap(gate), blank, up, swap(up), blank], 1)
    tall = jnp.concatenate([down, swap(down), jnp.zeros((pad, down.shape[1]), BF)], 0)
    return wide, tall


def hidden_kernel(count, rows_per_step, *refs):
    sources = refs[:count]
    wide, tall, into, joint, both, back, grads = refs[count : count + 7]
    step = pl.program_id(0)
    width = tall.shape[1]
    half = tall.shape[0]
    if count == 1:
        rows = sources[0]
    else:
        rows = refs[count + 7]
        size = sources[0].shape[0]
        each = rows_per_step // size
        for p in range(count):

            @pl.when(step == p // each)
            def _(p=p):
                rows[(p % each) * size : (p % each + 1) * size, :] = sources[p][...]

    tile = 256 if (2 * half) % 256 == 0 else 128

    def first(j, carry):
        cols = pl.ds(pl.multiple_of(j * tile, tile), tile)
        both[:, cols] = jnp.dot(rows[:, :width], wide[:, cols], preferred_element_type=F32)
        return carry

    lax.fori_loop(0, 2 * half // tile, first, 0)
    back[...] = lax.dot_general(
        rows[:, width:], tall[...], (((1,), (1,)), ((), ())), preferred_element_type=F32
    )
    gate, up, dy = both[:, :half], both[:, half:], back[...]
    sig = jax.nn.sigmoid(gate)
    active = gate * sig
    grad_up = dy * active
    grads[:, half:] = grad_up.astype(BF)
    grads[:, :half] = (dy * up * (sig + active * (1.0 - sig))).astype(BF)
    score = jnp.sum(grad_up * up, -1, keepdims=True)
    joint[...] = jnp.broadcast_to(score, joint.shape)
    block = 512 if width % 512 == 0 else 128

    def last(j, carry):
        cols = pl.ds(pl.multiple_of(j * block, block), block)
        into[:, cols] = lax.dot_general(
            grads[...], wide[cols, :], (((1,), (1,)), ((), ())), preferred_element_type=F32
        ).astype(BF)
        return carry

    lax.fori_loop(0, width // block, last, 0)


def hidden_grads(sources, wide, tall, step_rows):
    count = len(sources)
    size = sources[0].shape[0]
    total = count * size
    half, width = tall.shape
    steps = total // step_rows
    if count == 1:
        row_specs = [pl.BlockSpec((step_rows, 2 * width), lambda i: (i, 0))]
        extra = []
    else:
        row_specs = [
            pl.BlockSpec((size, 2 * width), lambda i: (0, 0), pipeline_mode=pl.Buffered(1))
        ] * count
        extra = [pltpu.VMEM((step_rows, 2 * width), BF)]

    def whole(shape):
        return pl.BlockSpec(shape, lambda i: (0, 0), pipeline_mode=pl.Buffered(1))

    into, joint = pl.pallas_call(
        lambda *refs: hidden_kernel(count, step_rows, *refs),
        grid=(steps,),
        in_specs=row_specs + [whole(wide.shape), whole(tall.shape)],
        out_specs=[
            pl.BlockSpec((step_rows, width), lambda i: (i, 0)),
            pl.BlockSpec((step_rows, 128), lambda i: (i, 0)),
        ],
        out_shape=[
            jax.ShapeDtypeStruct((total, width), BF),
            jax.ShapeDtypeStruct((total, 128), F32),
        ],
        scratch_shapes=[
            pltpu.VMEM((step_rows, 2 * half), F32),
            pltpu.VMEM((step_rows, half), F32),
            pltpu.VMEM((step_rows, 2 * half), BF),
        ]
        + extra,
        compiler_params=pltpu.CompilerParams(vmem_limit_bytes=VMEM_LIMIT),
        cost_estimate=pl.CostEstimate(
            flops=10 * total * width * half,
            bytes_accessed=6 * half * width + 6 * total * width,
            transcendentals=total * half,
        ),
    )(*sources, wide, tall)
    return into, joint[:, 0]


def pick_kernel(*refs):
    count = len(refs) // 2
    total = jnp.dot(refs[0][...], refs[count][...], preferred_element_type=F32)
    for i in range(1, count):
        total = total + jnp.dot(refs[i][...], refs[count + i][...], preferred_element_type=F32)
    refs[-1][...] = total.astype(BF)


def pick_rows(tables, sources):
    rows, tok = tables[0].shape
    width = sources[0].shape[1]
    block = 1024 if width % 1024 == 0 else 128
    count = len(sources)
    return pl.pallas_call(
        pick_kernel,
        grid=(width // block,),
        in_specs=[pl.BlockSpec((rows, tok), lambda i: (0, 0))] * count
        + [pl.BlockSpec((tok, block), lambda i: (0, i))] * count,
        out_specs=pl.BlockSpec((rows, block), lambda i: (0, i)),
        out_shape=jax.ShapeDtypeStruct((rows, width), BF),
        compiler_params=pltpu.CompilerParams(vmem_limit_bytes=VMEM_LIMIT),
        cost_estimate=pl.CostEstimate(
            flops=2 * count * rows * tok * width,
            bytes_accessed=2 * width * (rows + count * tok),
            transcendentals=0,
        ),
    )(*tables, *sources)


def slots_of(routes, experts):
    tok = routes.shape[0]
    flat = routes.reshape(2 * tok, 1)
    hits = (flat == lax.broadcasted_iota(jnp.int32, (1, experts), 1)).astype(BF)
    place = lax.broadcasted_iota(jnp.int32, (2 * tok, 2 * tok), 0)
    before = (lax.broadcasted_iota(jnp.int32, (2 * tok, 2 * tok), 1) < place).astype(BF)
    places = jnp.dot(before, hits, preferred_element_type=F32)
    return jnp.sum(hits.astype(F32) * places, -1).astype(jnp.int32).reshape(tok, 2)


def spread(index, rows):
    return index[..., None] == lax.broadcasted_iota(jnp.int32, (1, 1, rows), 2)


def picker(index, rows):
    hits = lax.broadcasted_iota(jnp.int32, (rows, 1), 0)
    return (hits == index[:, 0][None]).astype(BF) + (hits == index[:, 1][None]).astype(BF)


def router_weights(normed, router, chosen):
    logits = jnp.dot(normed.astype(F32), router, precision=HIGHEST)
    picked = jnp.sum(jnp.where(chosen, logits[:, None, :], 0.0), -1)
    one = jax.nn.sigmoid(picked[:, 0:1] - picked[:, 1:2])
    return jnp.concatenate([one, 1.0 - one], 1)


def mixer(hot, weights):
    return jnp.sum(jnp.where(hot, weights[..., None], 0.0), 1).astype(BF)


def body(
    tokens,
    cotangent,
    norm_gain,
    router,
    dense_gate,
    dense_up,
    dense_down,
    expert_gate,
    expert_up,
    expert_down,
    routes,
):
    tok, width = tokens.shape
    experts = router.shape[1]
    cap = 5 * tok // (2 * experts)
    own_rows = -(-cap // 8) * 8
    rest = cap - NEAR
    far_rows = -(-(cap + 2 * rest) // 8) * 8
    starts = {1: 0, 2: rest, 3: rest + cap}
    own_all = experts * own_rows
    far_all = experts * far_rows
    near_all = experts * NEAR
    none = -4 * far_all

    values = tokens.astype(F32)
    inverse = lax.rsqrt(jnp.mean(values * values, -1, keepdims=True) + EPS)
    normed = (values * inverse * norm_gain).astype(BF)
    pair = jnp.concatenate([normed, cotangent], 1)

    peer_routes = {k: receive_from(routes, k) for k in (1, 2, 3)}
    peer = {k: receive_from(pair, k) for k in (1, 2, 3)}
    own_index = routes * own_rows + slots_of(routes, experts)
    own = over(pick_rows([picker(own_index, own_all)], [pair]))

    far_index = {}
    for k in (1, 2, 3):
        slots = slots_of(peer_routes[k], experts)
        row = peer_routes[k] * far_rows + starts[k]
        if k == 2:
            far_index[k] = row + slots
        else:
            far_index[k] = jnp.where(slots >= NEAR, row + slots - NEAR, none)
    far_send = pick_rows(
        [picker(far_index[k], far_all) for k in (1, 2, 3)], [peer[k] for k in (1, 2, 3)]
    )
    far = over(far_send)
    near_send = own.reshape(experts, own_rows, 2 * width)[:, :NEAR].reshape(near_all, 2 * width)
    near1 = receive_from(near_send, 1)
    near3 = receive_from(near_send, 3)

    wide_e, tall_e = join_weights(expert_gate[0], expert_up[0], expert_down[0])
    wide_d, tall_d = join_weights(dense_gate, dense_up, dense_down)

    own_into, own_joint = hidden_grads(
        [after(own, far_send, near_send)], wide_e, tall_e, own_all // 2
    )
    dense_part, unused = hidden_grads(
        [after(pair, own_into)] + [peer[k] for k in (1, 2, 3)], wide_d, tall_d, 2 * tok
    )
    near_into, near_joint = hidden_grads(
        [after(near1, dense_part), near3], wide_e, tall_e, near_all
    )
    near1_back = send_to(near_into[:near_all], 1)
    near3_back = send_to(near_into[near_all:], 3)
    far_into, far_joint = hidden_grads([after(far, near_into)], wide_e, tall_e, far_all // 2)
    far_back = over(far_into)

    own_joint = own_joint.reshape(experts, own_rows)[:, :cap]
    near_joint = near_joint.reshape(2, experts, NEAR)
    far_joint = far_joint.reshape(experts, far_rows)
    joints = jnp.stack(
        [
            own_joint,
            jnp.concatenate([near_joint[0], far_joint[:, :rest]], 1),
            far_joint[:, starts[2] : starts[2] + cap],
            jnp.concatenate([near_joint[1], far_joint[:, starts[3] : starts[3] + rest]], 1),
        ],
        1,
    )
    plane = lax.broadcasted_iota(jnp.int32, (1, PEERS, PEERS, 1), 1)
    offset = lax.broadcasted_iota(jnp.int32, (1, PEERS, PEERS, 1), 2)
    meant = plane == (lax.axis_index("y") + offset) % PEERS
    joints = jnp.sum(jnp.where(meant, joints[:, None], 0.0), 2).reshape(experts * PEERS, cap)
    joints = over(after(joints, far_back), ("ep", "y"))
    score = jnp.sum(joints.reshape(experts, PEERS, cap), 1)

    near_back = near1_back.astype(F32) + near3_back.astype(F32)
    near_back = near_back.reshape(experts, NEAR, width)
    own_sum = own_into.astype(F32).reshape(experts, own_rows, width)
    own_sum = own_sum + jnp.pad(near_back, ((0, 0), (0, own_rows - NEAR), (0, 0)))
    own_sum = own_sum.astype(BF).reshape(own_all, width)
    own_back = over(after(own_sum, joints))

    ids = lax.broadcasted_iota(jnp.int32, (1, 1, experts), 2)
    chosen = routes[..., None] == ids
    weights = router_weights(normed, router, chosen)
    far_mix = []
    for k in (1, 2, 3):
        peer_weights = router_weights(peer[k][:, :width], router, peer_routes[k][..., None] == ids)
        far_mix.append(mixer(spread(far_index[k], far_all), peer_weights))
    mixed = jnp.dot(jnp.concatenate(far_mix, 0), far_back, preferred_element_type=F32)
    mixed = (mixed + dense_part[tok:].astype(F32)).astype(BF)
    home = [send_to(mixed[(k - 1) * tok : k * tok], k) for k in (2, 1, 3)]

    own_hot = spread(own_index, own_all)
    score = jnp.pad(score, ((0, 0), (0, own_rows - cap))).reshape(1, 1, -1)
    scores = jnp.sum(jnp.where(own_hot, score, 0.0), -1)
    delta = weights[:, 0] * weights[:, 1] * (scores[:, 0] - scores[:, 1])
    signed = chosen[:, 0].astype(F32) - chosen[:, 1].astype(F32)
    grad_logits = signed * delta[:, None]
    local_router = lax.dot_general(
        grad_logits, normed.astype(F32), (((0,), (0,)), ((), ())), precision=HIGHEST
    )
    early = dense_part[:tok].astype(F32)
    early = early + jnp.dot(grad_logits, router.T, precision=HIGHEST)

    own_mix = mixer(own_hot, weights)
    total = early + jnp.dot(own_mix, own_back, preferred_element_type=F32)
    for piece in home:
        total = total + piece.astype(F32)
    local_gain = jnp.sum(total * values * inverse, 0, keepdims=True)
    axes = ("ep", "y", "core")
    devices = lax.axis_size(axes)
    local = jnp.concatenate([local_router, local_gain], 0).reshape(devices, -1)
    mine = jnp.sum(over(local, axes), 0, keepdims=True)
    sums = over(jnp.broadcast_to(mine, local.shape), axes).reshape(experts + 1, width)
    scaled = total * norm_gain
    mean_term = jnp.mean(scaled * values, -1, keepdims=True)
    input_grad = cotangent.astype(F32) + inverse * (
        scaled - values * inverse * inverse * mean_term
    )
    return (input_grad.astype(BF), sums[experts], sums[:experts].T)


def solution(mesh):
    ep, sp = mesh.devices.shape
    grid = Mesh(mesh.devices.reshape(ep, sp // 2, 2), ("ep", "y", "core"))
    shared = ("y", "core")
    rows = ("ep", "y", "core")
    return jax.shard_map(
        body,
        mesh=grid,
        in_specs=(
            P(rows, None),
            P(rows, None),
            P(),
            P(),
            P(None, shared),
            P(None, shared),
            P(shared, None),
            P("ep", None, shared),
            P("ep", None, shared),
            P("ep", shared, None),
            P(rows, None),
        ),
        out_specs=(P(rows, None), P(), P()),
        check_vma=False,
    )
```

```python
import jax
import jax.numpy as jnp
from jax import lax
from jax.experimental import pallas as pl
from jax.experimental.pallas import tpu as pltpu
from jax.sharding import Mesh, PartitionSpec as P

EPS = 1e-05
BF = jnp.bfloat16
F32 = jnp.float32
HIGHEST = lax.Precision.HIGHEST
PEERS = 4
NEAR = 16
VMEM_LIMIT = 44 * 1024 * 1024
TRANS = (((1,), (1,)), ((), ()))


def receive_from(value, k):
    return lax.ppermute(value, "y", [(i, (i - k) % PEERS) for i in range(PEERS)])


def send_to(value, k):
    return lax.ppermute(value, "y", [(i, (i + k) % PEERS) for i in range(PEERS)])


def swap(value):
    return lax.ppermute(value, "core", [(0, 1), (1, 0)])


def over(value, axes="ep"):
    return lax.all_to_all(value, axes, split_axis=0, concat_axis=0, tiled=True)


def after(value, *others):
    return lax.optimization_barrier((value,) + others)[0]


def weight_pieces(gate, up, down):
    both = [gate.T, up.T, down]
    return [piece for value in both for piece in (value, swap(value))]


def hidden_kernel(count, rows_per_step, *refs):
    sources = refs[:count]
    pieces = refs[count : count + 6]
    into, joint, table, both, back, grads, sems = refs[count + 6 : count + 13]
    step = pl.program_id(0)
    part, width = pieces[0].shape
    half = table.shape[0] // 3
    copies = []
    for i in range(6):
        start = i // 2 * half + i % 2 * part
        copies.append(
            pltpu.make_async_copy(pieces[i], table.at[pl.ds(start, part), :], sems.at[i])
        )

    @pl.when(step == 0)
    def _():
        for copy in copies:
            copy.start()
        if half > 2 * part:
            for i in range(3):
                table[i * half + 2 * part : (i + 1) * half, :] = jnp.zeros(
                    (half - 2 * part, width), BF
                )

    if count == 1:
        rows = sources[0]
    else:
        rows = refs[count + 13]
        size = sources[0].shape[0]
        each = rows_per_step // size
        for p in range(count):

            @pl.when(step == p // each)
            def _(p=p):
                rows[(p % each) * size : (p % each + 1) * size, :] = sources[p][...]

    def wait(i, j):
        @pl.when(step == 0)
        def _():
            for copy in copies[i:j]:
                copy.wait()

    wait(0, 4)
    both[...] = lax.dot_general(
        rows[:, :width], table[: 2 * half, :], TRANS, preferred_element_type=F32
    )
    wait(4, 6)
    back[...] = lax.dot_general(
        rows[:, width:], table[2 * half :, :], TRANS, preferred_element_type=F32
    )
    gate, up, dy = both[:, :half], both[:, half:], back[...]
    sig = jax.nn.sigmoid(gate)
    active = gate * sig
    grad_up = dy * active
    grads[:, half:] = grad_up.astype(BF)
    grads[:, :half] = (dy * up * (sig + active * (1.0 - sig))).astype(BF)
    score = jnp.sum(grad_up * up, -1, keepdims=True)
    joint[...] = jnp.broadcast_to(score, joint.shape)
    into[...] = jnp.dot(
        grads[...], table[: 2 * half, :], preferred_element_type=F32
    ).astype(BF)


def hidden_grads(sources, pieces, step_rows):
    count = len(sources)
    size = sources[0].shape[0]
    total = count * size
    part, width = pieces[0].shape
    half = -(-2 * part // 128) * 128
    if count == 1:
        row_specs = [pl.BlockSpec((step_rows, 2 * width), lambda i: (i, 0))]
        extra = []
    else:
        row_specs = [
            pl.BlockSpec((size, 2 * width), lambda i: (0, 0), pipeline_mode=pl.Buffered(1))
        ] * count
        extra = [pltpu.VMEM((step_rows, 2 * width), BF)]
    into, joint = pl.pallas_call(
        lambda *refs: hidden_kernel(count, step_rows, *refs),
        grid=(total // step_rows,),
        in_specs=row_specs + [pl.BlockSpec(memory_space=pl.ANY)] * 6,
        out_specs=[
            pl.BlockSpec((step_rows, width), lambda i: (i, 0)),
            pl.BlockSpec((step_rows, 128), lambda i: (i, 0)),
        ],
        out_shape=[
            jax.ShapeDtypeStruct((total, width), BF),
            jax.ShapeDtypeStruct((total, 128), F32),
        ],
        scratch_shapes=[
            pltpu.VMEM((3 * half, width), BF),
            pltpu.VMEM((step_rows, 2 * half), F32),
            pltpu.VMEM((step_rows, half), F32),
            pltpu.VMEM((step_rows, 2 * half), BF),
            pltpu.SemaphoreType.DMA((6,)),
        ]
        + extra,
        compiler_params=pltpu.CompilerParams(vmem_limit_bytes=VMEM_LIMIT),
        cost_estimate=pl.CostEstimate(
            flops=10 * total * width * half,
            bytes_accessed=6 * half * width + 6 * total * width,
            transcendentals=total * half,
        ),
    )(*sources, *pieces)
    return into, joint[:, 0]


def pick_kernel(count, *refs):
    table, sources, out = refs[0], refs[1 : 1 + count], refs[1 + count]
    if count == 1:
        rows = sources[0][...]
    else:
        tall = refs[2 + count]
        tok = sources[0].shape[0]
        for i in range(count):
            tall[i * tok : (i + 1) * tok, :] = sources[i][...]
        rows = tall[...]
    out[...] = jnp.dot(table[...], rows, preferred_element_type=F32).astype(BF)


def pick_rows(table, sources, block=1024):
    rows, depth = table.shape
    tok, width = sources[0].shape
    block = block if width % block == 0 else 128
    count = len(sources)
    return pl.pallas_call(
        lambda *refs: pick_kernel(count, *refs),
        grid=(width // block,),
        in_specs=[pl.BlockSpec((rows, depth), lambda i: (0, 0))]
        + [pl.BlockSpec((tok, block), lambda i: (0, i))] * count,
        out_specs=pl.BlockSpec((rows, block), lambda i: (0, i)),
        out_shape=jax.ShapeDtypeStruct((rows, width), BF),
        scratch_shapes=[pltpu.VMEM((depth, block), BF)] if count > 1 else [],
        compiler_params=pltpu.CompilerParams(vmem_limit_bytes=VMEM_LIMIT),
        cost_estimate=pl.CostEstimate(
            flops=2 * rows * depth * width,
            bytes_accessed=2 * width * (rows + depth),
            transcendentals=0,
        ),
    )(table, *sources)


def slots_of(routes, experts):
    tok = routes.shape[0]
    flat = routes.reshape(2 * tok, 1)
    hits = (flat == lax.broadcasted_iota(jnp.int32, (1, experts), 1)).astype(BF)
    place = lax.broadcasted_iota(jnp.int32, (2 * tok, 2 * tok), 0)
    before = (lax.broadcasted_iota(jnp.int32, (2 * tok, 2 * tok), 1) < place).astype(BF)
    places = jnp.dot(before, hits, preferred_element_type=F32)
    return jnp.sum(hits.astype(F32) * places, -1).astype(jnp.int32).reshape(tok, 2)


def spread(index, rows):
    return index[..., None] == lax.broadcasted_iota(jnp.int32, (1, 1, rows), 2)


def picker(index, rows):
    hits = lax.broadcasted_iota(jnp.int32, (rows, 1), 0)
    return (hits == index[:, 0][None]).astype(BF) + (hits == index[:, 1][None]).astype(BF)


def router_weights(normed, router, chosen):
    logits = jnp.dot(normed.astype(F32), router, precision=HIGHEST)
    picked = jnp.sum(jnp.where(chosen, logits[:, None, :], 0.0), -1)
    one = jax.nn.sigmoid(picked[:, 0:1] - picked[:, 1:2])
    return jnp.concatenate([one, 1.0 - one], 1)


def mixer(hot, weights):
    return jnp.sum(jnp.where(hot, weights[..., None], 0.0), 1).astype(BF)


def body(
    tokens,
    cotangent,
    norm_gain,
    router,
    dense_gate,
    dense_up,
    dense_down,
    expert_gate,
    expert_up,
    expert_down,
    routes,
):
    tok, width = tokens.shape
    experts = router.shape[1]
    cap = 5 * tok // (2 * experts)
    own_rows = -(-cap // 8) * 8
    rest = cap - NEAR
    far_rows = -(-(cap + 2 * rest) // 8) * 8
    starts = {1: 0, 2: rest, 3: rest + cap}
    own_all = experts * own_rows
    far_all = experts * far_rows
    near_all = experts * NEAR
    none = -4 * far_all

    values = tokens.astype(F32)
    inverse = lax.rsqrt(jnp.mean(values * values, -1, keepdims=True) + EPS)
    normed = (values * inverse * norm_gain).astype(BF)
    pair = jnp.concatenate([normed, cotangent], 1)

    peer_routes = {k: receive_from(routes, k) for k in (1, 2, 3)}
    peer = {k: receive_from(pair, k) for k in (1, 2, 3)}
    known = after(routes, *peer_routes.values())
    own_index = known * own_rows + slots_of(known, experts)
    own = over(pick_rows(picker(own_index, own_all), [pair]))

    far_index = {}
    for k in (1, 2, 3):
        slots = slots_of(peer_routes[k], experts)
        row = peer_routes[k] * far_rows + starts[k]
        if k == 2:
            far_index[k] = row + slots
        else:
            far_index[k] = jnp.where(slots >= NEAR, row + slots - NEAR, none)
    far_table = jnp.concatenate([far_index[k] for k in (1, 2, 3)], 0)
    far_send = pick_rows(picker(far_table, far_all), [peer[k] for k in (1, 2, 3)])
    far = over(far_send)
    near_send = own.reshape(experts, own_rows, 2 * width)[:, :NEAR].reshape(near_all, 2 * width)
    near1 = receive_from(near_send, 1)
    near3 = receive_from(near_send, 3)

    expert = weight_pieces(expert_gate[0], expert_up[0], expert_down[0])
    dense = weight_pieces(dense_gate, dense_up, dense_down)

    own_into, own_joint = hidden_grads(
        [after(own, far_send, near_send)], expert, own_all
    )
    dense_part, unused = hidden_grads(
        [after(pair, own_into)] + [peer[k] for k in (1, 2, 3)], dense, 2 * tok
    )
    near_into, near_joint = hidden_grads(
        [after(near1, dense_part), near3], expert, near_all
    )
    near1_back = send_to(near_into[:near_all], 1)
    near3_back = send_to(near_into[near_all:], 3)
    far_into, far_joint = hidden_grads([after(far, near_into)], expert, far_all // 2)
    far_back = over(far_into)

    own_joint = own_joint.reshape(experts, own_rows)[:, :cap]
    near_joint = near_joint.reshape(2, experts, NEAR)
    far_joint = far_joint.reshape(experts, far_rows)
    joints = jnp.stack(
        [
            own_joint,
            jnp.concatenate([near_joint[0], far_joint[:, :rest]], 1),
            far_joint[:, starts[2] : starts[2] + cap],
            jnp.concatenate([near_joint[1], far_joint[:, starts[3] : starts[3] + rest]], 1),
        ],
        1,
    )
    plane = lax.broadcasted_iota(jnp.int32, (1, PEERS, PEERS, 1), 1)
    offset = lax.broadcasted_iota(jnp.int32, (1, PEERS, PEERS, 1), 2)
    meant = plane == (lax.axis_index("y") + offset) % PEERS
    joints = jnp.sum(jnp.where(meant, joints[:, None], 0.0), 2).reshape(experts * PEERS, cap)
    joints = over(after(joints, far_back), ("ep", "y"))
    score = jnp.sum(joints.reshape(experts, PEERS, cap), 1)

    near_back = near1_back.astype(F32) + near3_back.astype(F32)
    near_back = near_back.reshape(experts, NEAR, width)
    own_sum = own_into.astype(F32).reshape(experts, own_rows, width)
    own_sum = own_sum + jnp.pad(near_back, ((0, 0), (0, own_rows - NEAR), (0, 0)))
    own_sum = own_sum.astype(BF).reshape(own_all, width)
    own_back = over(after(own_sum, joints))

    ids = lax.broadcasted_iota(jnp.int32, (1, 1, experts), 2)
    chosen = routes[..., None] == ids
    weights = router_weights(normed, router, chosen)
    far_mix = []
    for k in (1, 2, 3):
        peer_weights = router_weights(peer[k][:, :width], router, peer_routes[k][..., None] == ids)
        far_mix.append(mixer(spread(far_index[k], far_all), peer_weights))
    mixed = jnp.dot(jnp.concatenate(far_mix, 0), far_back, preferred_element_type=F32)
    mixed = (mixed + dense_part[tok:].astype(F32)).astype(BF)
    home = [send_to(mixed[(k - 1) * tok : k * tok], k) for k in (2, 1, 3)]

    own_hot = spread(own_index, own_all)
    score = jnp.pad(score, ((0, 0), (0, own_rows - cap))).reshape(1, 1, -1)
    scores = jnp.sum(jnp.where(own_hot, score, 0.0), -1)
    delta = weights[:, 0] * weights[:, 1] * (scores[:, 0] - scores[:, 1])
    signed = chosen[:, 0].astype(F32) - chosen[:, 1].astype(F32)
    grad_logits = signed * delta[:, None]
    local_router = lax.dot_general(
        grad_logits, normed.astype(F32), (((0,), (0,)), ((), ())), precision=HIGHEST
    )
    early = dense_part[:tok].astype(F32)
    early = early + jnp.dot(grad_logits, router.T, precision=HIGHEST)

    own_mix = mixer(own_hot, weights)
    total = early + jnp.dot(own_mix, own_back, preferred_element_type=F32)
    for piece in home:
        total = total + piece.astype(F32)
    local_gain = jnp.sum(total * values * inverse, 0, keepdims=True)
    axes = ("ep", "y", "core")
    devices = lax.axis_size(axes)
    local = jnp.concatenate([local_router, local_gain], 0).reshape(devices, -1)
    mine = jnp.sum(over(local, axes), 0, keepdims=True)
    sums = over(jnp.broadcast_to(mine, local.shape), axes).reshape(experts + 1, width)
    scaled = total * norm_gain
    mean_term = jnp.mean(scaled * values, -1, keepdims=True)
    input_grad = cotangent.astype(F32) + inverse * (
        scaled - values * inverse * inverse * mean_term
    )
    return (input_grad.astype(BF), sums[experts], sums[:experts].T)


def solution(mesh):
    ep, sp = mesh.devices.shape
    grid = Mesh(mesh.devices.reshape(ep, sp // 2, 2), ("ep", "y", "core"))
    shared = ("y", "core")
    rows = ("ep", "y", "core")
    return jax.shard_map(
        body,
        mesh=grid,
        in_specs=(
            P(rows, None),
            P(rows, None),
            P(),
            P(),
            P(None, shared),
            P(None, shared),
            P(shared, None),
            P("ep", None, shared),
            P("ep", None, shared),
            P("ep", shared, None),
            P(rows, None),
        ),
        out_specs=(P(rows, None), P(), P()),
        check_vma=False,
    )
```

```python
import jax
import jax.numpy as jnp
from jax import lax
from jax.experimental import pallas as pl
from jax.experimental.pallas import tpu as pltpu
from jax.sharding import Mesh, PartitionSpec as P

EPS = 1e-05
BF = jnp.bfloat16
F32 = jnp.float32
HIGHEST = lax.Precision.HIGHEST
PEERS = 4
VMEM_LIMIT = 50 * 1024 * 1024
TRANS = (((1,), (1,)), ((), ()))


def receive_from(value, k):
    return lax.ppermute(value, "y", [(i, (i - k) % PEERS) for i in range(PEERS)])


def send_to(value, k):
    return lax.ppermute(value, "y", [(i, (i + k) % PEERS) for i in range(PEERS)])


def swap(value):
    return lax.ppermute(value, "core", [(0, 1), (1, 0)])


def over(value, axes="ep"):
    return lax.all_to_all(value, axes, split_axis=0, concat_axis=0, tiled=True)


def after(value, *others):
    return lax.optimization_barrier((value,) + others)[0]


def weight_pieces(gate, up, down):
    both = [gate.T, up.T, down]
    return [piece for value in both for piece in (value, swap(value))]


def shuffle_table(cap, group):
    size = 2 * group * cap
    row = lax.broadcasted_iota(jnp.int32, (size, size), 0)
    col = lax.broadcasted_iota(jnp.int32, (size, size), 1)
    part, left = row // (group * cap), row % (group * cap)
    return (col == left // cap * (2 * cap) + part * cap + left % cap).astype(BF)


def hidden_kernel(count, mixed, *refs):
    sources = refs[:count]
    pieces = refs[count : count + 6]
    refs = refs[count + 6 :]
    if mixed:
        table, table_back = refs[:2]
        refs = refs[2:]
    into, joint, weights, normed, other, both, back, grads, sems = refs
    step = pl.program_id(0)
    part, width = pieces[0].shape
    half = weights.shape[0] // 3
    copies = []
    for i in range(6):
        start = i // 2 * half + i % 2 * part
        copies.append(
            pltpu.make_async_copy(pieces[i], weights.at[pl.ds(start, part), :], sems.at[i])
        )

    @pl.when(step == 0)
    def _():
        for copy in copies:
            copy.start()
        if half > 2 * part:
            for i in range(3):
                weights[i * half + 2 * part : (i + 1) * half, :] = jnp.zeros(
                    (half - 2 * part, width), BF
                )

    size = sources[0].shape[0] // 2
    each = normed.shape[0] // size
    for p in range(count):

        @pl.when(step == p // each)
        def _(p=p):
            if mixed:
                chunk = table.shape[0]
                for i in range(2 * size // chunk):
                    got = jnp.dot(
                        table[...],
                        sources[p][i * chunk : (i + 1) * chunk, :],
                        preferred_element_type=F32,
                    ).astype(BF)
                    at = slice(i * chunk // 2, (i + 1) * chunk // 2)
                    normed[at, :] = got[: chunk // 2]
                    other[at, :] = got[chunk // 2 :]
            else:
                at = slice((p % each) * size, (p % each + 1) * size)
                normed[at, :] = sources[p][:size, :]
                other[at, :] = sources[p][size:, :]

    def wait(i, j):
        @pl.when(step == 0)
        def _():
            for copy in copies[i:j]:
                copy.wait()

    wait(0, 4)
    both[...] = lax.dot_general(
        normed[...], weights[: 2 * half, :], TRANS, preferred_element_type=F32
    )
    wait(4, 6)
    back[...] = lax.dot_general(
        other[...], weights[2 * half :, :], TRANS, preferred_element_type=F32
    )
    gate, up, dy = both[:, :half], both[:, half:], back[...]
    sig = jax.nn.sigmoid(gate)
    active = gate * sig
    grad_up = dy * active
    grads[:, half:] = grad_up.astype(BF)
    grads[:, :half] = (dy * up * (sig + active * (1.0 - sig))).astype(BF)
    score = jnp.sum(grad_up * up, -1, keepdims=True)
    joint[...] = jnp.broadcast_to(score, joint.shape)
    if mixed:
        other[...] = jnp.dot(
            grads[...], weights[: 2 * half, :], preferred_element_type=F32
        ).astype(BF)
        chunk = table.shape[0]
        for i in range(2 * size // chunk):
            at = slice(i * chunk // 2, (i + 1) * chunk // 2)
            sides = jnp.concatenate([other[at, : width // 2], other[at, width // 2 :]], 0)
            into[i * chunk : (i + 1) * chunk, :] = jnp.dot(
                table_back[...], sides, preferred_element_type=F32
            ).astype(BF)
    else:
        into[...] = jnp.dot(
            grads[...], weights[: 2 * half, :], preferred_element_type=F32
        ).astype(BF)


def hidden_grads(sources, pieces, tables=()):
    count = len(sources)
    mixed = len(tables) > 0
    size = sources[0].shape[0] // 2
    part, width = pieces[0].shape
    half = -(-2 * part // 128) * 128
    step_rows = size if mixed else 2 * size
    total = count * size
    out = (2 * total, width // 2) if mixed else (total, width)
    block = (2 * step_rows, width // 2) if mixed else (step_rows, width)

    def whole(value):
        return pl.BlockSpec(value.shape, lambda i: (0, 0), pipeline_mode=pl.Buffered(1))

    into, joint = pl.pallas_call(
        lambda *refs: hidden_kernel(count, mixed, *refs),
        grid=(total // step_rows,),
        in_specs=[whole(v) for v in sources]
        + [pl.BlockSpec(memory_space=pl.ANY)] * 6
        + [whole(v) for v in tables],
        out_specs=[
            pl.BlockSpec(block, lambda i: (i, 0)),
            pl.BlockSpec((step_rows, 128), lambda i: (i, 0)),
        ],
        out_shape=[jax.ShapeDtypeStruct(out, BF), jax.ShapeDtypeStruct((total, 128), F32)],
        scratch_shapes=[
            pltpu.VMEM((3 * half, width), BF),
            pltpu.VMEM((step_rows, width), BF),
            pltpu.VMEM((step_rows, width), BF),
            pltpu.VMEM((step_rows, 2 * half), F32),
            pltpu.VMEM((step_rows, half), F32),
            pltpu.VMEM((step_rows, 2 * half), BF),
            pltpu.SemaphoreType.DMA((6,)),
        ],
        compiler_params=pltpu.CompilerParams(vmem_limit_bytes=VMEM_LIMIT),
        cost_estimate=pl.CostEstimate(
            flops=10 * total * width * half,
            bytes_accessed=6 * half * width + 6 * total * width,
            transcendentals=total * half,
        ),
    )(*sources, *pieces, *tables)
    return into, joint[:, 0]


def pick_kernel(table, rows, out):
    out[...] = jnp.dot(table[...], rows[...], preferred_element_type=F32).astype(BF)


def pick_rows(table, source):
    rows, depth = table.shape
    width = source.shape[1]
    block = 512 if width % 512 == 0 else 128
    return pl.pallas_call(
        pick_kernel,
        grid=(width // block,),
        in_specs=[
            pl.BlockSpec((rows, depth), lambda i: (0, 0)),
            pl.BlockSpec((depth, block), lambda i: (0, i)),
        ],
        out_specs=pl.BlockSpec((rows, block), lambda i: (0, i)),
        out_shape=jax.ShapeDtypeStruct((rows, width), BF),
        compiler_params=pltpu.CompilerParams(vmem_limit_bytes=VMEM_LIMIT),
        cost_estimate=pl.CostEstimate(
            flops=2 * rows * depth * width,
            bytes_accessed=2 * width * (rows + depth),
            transcendentals=0,
        ),
    )(table, source)


def slots_of(routes, experts):
    tok = routes.shape[0]
    flat = routes.reshape(2 * tok, 1)
    hits = (flat == lax.broadcasted_iota(jnp.int32, (1, experts), 1)).astype(BF)
    place = lax.broadcasted_iota(jnp.int32, (2 * tok, 2 * tok), 0)
    before = (lax.broadcasted_iota(jnp.int32, (2 * tok, 2 * tok), 1) < place).astype(BF)
    places = jnp.dot(before, hits, preferred_element_type=F32)
    return jnp.sum(hits.astype(F32) * places, -1).astype(jnp.int32).reshape(tok, 2)


def spread(index, rows):
    return index[..., None] == lax.broadcasted_iota(jnp.int32, (1, 1, rows), 2)


def picker(index, rows):
    hits = lax.broadcasted_iota(jnp.int32, (rows, 1), 0)
    return (hits == index[:, 0][None]).astype(BF) + (hits == index[:, 1][None]).astype(BF)


def router_weights(normed, router, chosen):
    logits = jnp.dot(normed.astype(F32), router, precision=HIGHEST)
    picked = jnp.sum(jnp.where(chosen, logits[:, None, :], 0.0), -1)
    one = jax.nn.sigmoid(picked[:, 0:1] - picked[:, 1:2])
    return jnp.concatenate([one, 1.0 - one], 1)


def mix(index, weights, rows, cap):
    count = rows.shape[0]
    tables = []
    for shift in (0, cap):
        hot = spread(index + shift, count)
        tables.append(jnp.sum(jnp.where(hot, weights[..., None], 0.0), 1).astype(BF))
    tok = index.shape[0]
    sides = jnp.dot(jnp.concatenate(tables, 0), rows, preferred_element_type=F32)
    return jnp.concatenate([sides[:tok], sides[tok:]], 1)


def body(
    tokens,
    cotangent,
    norm_gain,
    router,
    dense_gate,
    dense_up,
    dense_down,
    expert_gate,
    expert_up,
    expert_down,
    routes,
):
    tok, width = tokens.shape
    experts = router.shape[1]
    cap = 5 * tok // (2 * experts)
    block = 2 * cap
    everything = experts * block

    values = tokens.astype(F32)
    inverse = lax.rsqrt(jnp.mean(values * values, -1, keepdims=True) + EPS)
    normed = (values * inverse * norm_gain).astype(BF)
    pair = jnp.concatenate([normed, cotangent], 0)

    routes_in = after(routes, pair)
    peer_routes = {k: receive_from(routes_in, k) for k in (1, 2, 3)}
    peer = {k: receive_from(pair, k) for k in (1, 2, 3)}

    def to_experts(rows, index):
        places = jnp.concatenate([index, index + cap], 0)
        return over(pick_rows(picker(places, everything), rows))

    known = after(routes, *peer_routes.values())
    own_index = known * block + slots_of(known, experts)
    far_index = peer_routes[2] * block + slots_of(peer_routes[2], experts)
    own = to_experts(pair, own_index)
    far = to_experts(peer[2], far_index)
    near1 = receive_from(own, 1)
    near3 = receive_from(own, 3)

    expert = weight_pieces(expert_gate[0], expert_up[0], expert_down[0])
    dense = weight_pieces(dense_gate, dense_up, dense_down)
    table = shuffle_table(cap, experts // 2)
    tables = (table, table.T)

    own_into, own_joint = hidden_grads([own], expert, tables)
    dense_part, unused = hidden_grads(
        [after(pair, own_into)] + [peer[k] for k in (1, 2, 3)], dense
    )
    far_into, far_joint = hidden_grads([after(far, dense_part)], expert, tables)
    far_back = over(far_into)
    near_into, near_joint = hidden_grads([after(near1, far_into), near3], expert, tables)
    home1 = send_to(after(dense_part[tok : 2 * tok], near1), 1)
    home3 = send_to(after(dense_part[3 * tok :], near3), 3)
    near_into = after(near_into, home1, home3)
    near1_back = send_to(near_into[:everything], 1)
    near3_back = send_to(near_into[everything:], 3)

    joints = jnp.stack(
        [
            own_joint.reshape(experts, cap),
            near_joint[: experts * cap].reshape(experts, cap),
            far_joint.reshape(experts, cap),
            near_joint[experts * cap :].reshape(experts, cap),
        ],
        1,
    )
    plane = lax.broadcasted_iota(jnp.int32, (1, PEERS, PEERS, 1), 1)
    offset = lax.broadcasted_iota(jnp.int32, (1, PEERS, PEERS, 1), 2)
    meant = plane == (lax.axis_index("y") + offset) % PEERS
    joints = jnp.sum(jnp.where(meant, joints[:, None], 0.0), 2).reshape(experts * PEERS, cap)
    joints = over(after(joints, far_back), ("ep", "y"))
    score = jnp.sum(joints.reshape(experts, PEERS, cap), 1)

    own_sum = own_into.astype(F32) + near1_back.astype(F32) + near3_back.astype(F32)
    own_back = over(after(own_sum.astype(BF), joints))

    ids = lax.broadcasted_iota(jnp.int32, (1, 1, experts), 2)
    chosen = routes[..., None] == ids
    weights = router_weights(normed, router, chosen)
    far_weights = router_weights(peer[2][:tok], router, peer_routes[2][..., None] == ids)
    mixed = dense_part[2 * tok : 3 * tok].astype(F32)
    mixed = mixed + mix(far_index, far_weights, far_back, cap)
    home2 = send_to(mixed.astype(BF), 2)

    scores = jnp.sum(
        jnp.where(
            spread(routes * cap + own_index - routes * block, experts * cap),
            score.reshape(1, 1, -1),
            0.0,
        ),
        -1,
    )
    delta = weights[:, 0] * weights[:, 1] * (scores[:, 0] - scores[:, 1])
    signed = chosen[:, 0].astype(F32) - chosen[:, 1].astype(F32)
    grad_logits = signed * delta[:, None]
    local_router = lax.dot_general(
        grad_logits, normed.astype(F32), (((0,), (0,)), ((), ())), precision=HIGHEST
    )
    early = dense_part[:tok].astype(F32)
    early = early + jnp.dot(grad_logits, router.T, precision=HIGHEST)
    for piece in (home1, home3):
        early = early + piece.astype(F32)

    total = early + home2.astype(F32) + mix(own_index, weights, own_back, cap)
    local_gain = jnp.sum(total * values * inverse, 0, keepdims=True)
    axes = ("ep", "y", "core")
    devices = lax.axis_size(axes)
    local = jnp.concatenate([local_router, local_gain], 0).reshape(devices, -1)
    mine = jnp.sum(over(local, axes), 0, keepdims=True)
    sums = over(jnp.broadcast_to(mine, local.shape), axes).reshape(experts + 1, width)
    scaled = total * norm_gain
    mean_term = jnp.mean(scaled * values, -1, keepdims=True)
    input_grad = cotangent.astype(F32) + inverse * (
        scaled - values * inverse * inverse * mean_term
    )
    return (input_grad.astype(BF), sums[experts], sums[:experts].T)


def solution(mesh):
    ep, sp = mesh.devices.shape
    grid = Mesh(mesh.devices.reshape(ep, sp // 2, 2), ("ep", "y", "core"))
    shared = ("y", "core")
    rows = ("ep", "y", "core")
    return jax.shard_map(
        body,
        mesh=grid,
        in_specs=(
            P(rows, None),
            P(rows, None),
            P(),
            P(),
            P(None, shared),
            P(None, shared),
            P(shared, None),
            P("ep", None, shared),
            P("ep", None, shared),
            P("ep", shared, None),
            P(rows, None),
        ),
        out_specs=(P(rows, None), P(), P()),
        check_vma=False,
    )
```

```python
import jax
import jax.numpy as jnp
from jax import lax
from jax.experimental import pallas as pl
from jax.experimental.pallas import tpu as pltpu
from jax.sharding import Mesh, PartitionSpec as P

EPS = 1e-05
BF = jnp.bfloat16
F32 = jnp.float32
HIGHEST = lax.Precision.HIGHEST
PEERS = 4
VMEM_LIMIT = 50 * 1024 * 1024
TRANS = (((1,), (1,)), ((), ()))


def receive_from(value, k):
    return lax.ppermute(value, "y", [(i, (i - k) % PEERS) for i in range(PEERS)])


def send_to(value, k):
    return lax.ppermute(value, "y", [(i, (i + k) % PEERS) for i in range(PEERS)])


def swap(value):
    return lax.ppermute(value, "core", [(0, 1), (1, 0)])


def over(value, axes="ep"):
    return lax.all_to_all(value, axes, split_axis=0, concat_axis=0, tiled=True)


def after(value, *others):
    return lax.optimization_barrier((value,) + others)[0]


def weight_pieces(gate, up, down):
    both = [gate.T, up.T, down]
    return [piece for value in both for piece in (value, swap(value))]


def shuffle_table(cap, group):
    size = 2 * group * cap
    row = lax.broadcasted_iota(jnp.int32, (size, size), 0)
    col = lax.broadcasted_iota(jnp.int32, (size, size), 1)
    part, left = row // (group * cap), row % (group * cap)
    return (col == left // cap * (2 * cap) + part * cap + left % cap).astype(BF)


def hidden_kernel(count, mixed, *refs):
    sources = refs[:count]
    pieces = refs[count : count + 6]
    refs = refs[count + 6 :]
    if mixed:
        table, table_back = refs[:2]
        refs = refs[2:]
    into, joint, weights, normed, other, both, back, grads, sems = refs
    step = pl.program_id(0)
    part, width = pieces[0].shape
    half = weights.shape[0] // 3
    copies = []
    for i in range(6):
        start = i // 2 * half + i % 2 * part
        copies.append(
            pltpu.make_async_copy(pieces[i], weights.at[pl.ds(start, part), :], sems.at[i])
        )

    @pl.when(step == 0)
    def _():
        for copy in copies[4:] + copies[:4]:
            copy.start()
        if half > 2 * part:
            for i in range(3):
                weights[i * half + 2 * part : (i + 1) * half, :] = jnp.zeros(
                    (half - 2 * part, width), BF
                )

    size = sources[0].shape[0] // 2
    each = normed.shape[0] // size
    for p in range(count):

        @pl.when(step == p // each)
        def _(p=p):
            first = p % each * size
            if mixed:
                chunk = table.shape[0]
                for i in range(2 * size // chunk):
                    got = jnp.dot(
                        table[...],
                        sources[p][i * chunk : (i + 1) * chunk, :],
                        preferred_element_type=F32,
                    ).astype(BF)
                    at = slice(first + i * chunk // 2, first + (i + 1) * chunk // 2)
                    normed[at, :] = got[: chunk // 2]
                    other[at, :] = got[chunk // 2 :]
            else:
                at = slice(first, first + size)
                normed[at, :] = sources[p][:size, :]
                other[at, :] = sources[p][size:, :]

    def wait(i, j):
        @pl.when(step == 0)
        def _():
            for copy in copies[i:j]:
                copy.wait()

    wait(4, 6)
    back[...] = lax.dot_general(
        other[...], weights[2 * half :, :], TRANS, preferred_element_type=F32
    )
    wait(0, 4)
    both[...] = lax.dot_general(
        normed[...], weights[: 2 * half, :], TRANS, preferred_element_type=F32
    )
    gate, up, dy = both[:, :half], both[:, half:], back[...]
    sig = jax.nn.sigmoid(gate)
    active = gate * sig
    grad_up = dy * active
    grads[:, half:] = grad_up.astype(BF)
    grads[:, :half] = (dy * up * (sig + active * (1.0 - sig))).astype(BF)
    score = jnp.sum(grad_up * up, -1, keepdims=True)
    joint[...] = jnp.broadcast_to(score, joint.shape)
    if mixed:
        other[...] = jnp.dot(
            grads[...], weights[: 2 * half, :], preferred_element_type=F32
        ).astype(BF)
        chunk = table.shape[0]
        for i in range(2 * normed.shape[0] // chunk):
            at = slice(i * chunk // 2, (i + 1) * chunk // 2)
            sides = jnp.concatenate([other[at, : width // 2], other[at, width // 2 :]], 0)
            into[i * chunk : (i + 1) * chunk, :] = jnp.dot(
                table_back[...], sides, preferred_element_type=F32
            ).astype(BF)
    else:
        into[...] = jnp.dot(
            grads[...], weights[: 2 * half, :], preferred_element_type=F32
        ).astype(BF)


def hidden_grads(sources, pieces, tables=()):
    count = len(sources)
    mixed = len(tables) > 0
    size = sources[0].shape[0] // 2
    part, width = pieces[0].shape
    half = -(-2 * part // 128) * 128
    total = count * size
    step_rows = min(total, 320) if mixed else 2 * size
    out = (2 * total, width // 2) if mixed else (total, width)
    block = (2 * step_rows, width // 2) if mixed else (step_rows, width)

    def whole(value):
        return pl.BlockSpec(value.shape, lambda i: (0, 0), pipeline_mode=pl.Buffered(1))

    into, joint = pl.pallas_call(
        lambda *refs: hidden_kernel(count, mixed, *refs),
        grid=(total // step_rows,),
        in_specs=[whole(v) for v in sources]
        + [pl.BlockSpec(memory_space=pl.ANY)] * 6
        + [whole(v) for v in tables],
        out_specs=[
            pl.BlockSpec(block, lambda i: (i, 0)),
            pl.BlockSpec((step_rows, 128), lambda i: (i, 0)),
        ],
        out_shape=[jax.ShapeDtypeStruct(out, BF), jax.ShapeDtypeStruct((total, 128), F32)],
        scratch_shapes=[
            pltpu.VMEM((3 * half, width), BF),
            pltpu.VMEM((step_rows, width), BF),
            pltpu.VMEM((step_rows, width), BF),
            pltpu.VMEM((step_rows, 2 * half), F32),
            pltpu.VMEM((step_rows, half), F32),
            pltpu.VMEM((step_rows, 2 * half), BF),
            pltpu.SemaphoreType.DMA((6,)),
        ],
        compiler_params=pltpu.CompilerParams(vmem_limit_bytes=VMEM_LIMIT),
        cost_estimate=pl.CostEstimate(
            flops=10 * total * width * half,
            bytes_accessed=6 * half * width + 6 * total * width,
            transcendentals=total * half,
        ),
    )(*sources, *pieces, *tables)
    return into, joint[:, 0]


def pick_kernel(table, rows, out):
    out[...] = jnp.dot(table[...], rows[...], preferred_element_type=F32).astype(BF)


def pick_rows(table, source):
    rows, depth = table.shape
    width = source.shape[1]
    block = 512 if width % 512 == 0 else 128
    return pl.pallas_call(
        pick_kernel,
        grid=(width // block,),
        in_specs=[
            pl.BlockSpec((rows, depth), lambda i: (0, 0)),
            pl.BlockSpec((depth, block), lambda i: (0, i)),
        ],
        out_specs=pl.BlockSpec((rows, block), lambda i: (0, i)),
        out_shape=jax.ShapeDtypeStruct((rows, width), BF),
        compiler_params=pltpu.CompilerParams(vmem_limit_bytes=VMEM_LIMIT),
        cost_estimate=pl.CostEstimate(
            flops=2 * rows * depth * width,
            bytes_accessed=2 * width * (rows + depth),
            transcendentals=0,
        ),
    )(table, source)


def slots_of(routes, experts):
    tok = routes.shape[0]
    flat = routes.reshape(2 * tok, 1)
    hits = (flat == lax.broadcasted_iota(jnp.int32, (1, experts), 1)).astype(BF)
    place = lax.broadcasted_iota(jnp.int32, (2 * tok, 2 * tok), 0)
    before = (lax.broadcasted_iota(jnp.int32, (2 * tok, 2 * tok), 1) < place).astype(BF)
    places = jnp.dot(before, hits, preferred_element_type=F32)
    return jnp.sum(hits.astype(F32) * places, -1).astype(jnp.int32).reshape(tok, 2)


def spread(index, rows):
    return index[..., None] == lax.broadcasted_iota(jnp.int32, (1, 1, rows), 2)


def picker(index, rows):
    hits = lax.broadcasted_iota(jnp.int32, (rows, 1), 0)
    return (hits == index[:, 0][None]).astype(BF) + (hits == index[:, 1][None]).astype(BF)


def router_weights(normed, router, chosen):
    logits = jnp.dot(normed.astype(F32), router, precision=HIGHEST)
    picked = jnp.sum(jnp.where(chosen, logits[:, None, :], 0.0), -1)
    one = jax.nn.sigmoid(picked[:, 0:1] - picked[:, 1:2])
    return jnp.concatenate([one, 1.0 - one], 1)


def mix(index, weights, rows, cap):
    count = rows.shape[0]
    tables = []
    for shift in (0, cap):
        hot = spread(index + shift, count)
        tables.append(jnp.sum(jnp.where(hot, weights[..., None], 0.0), 1).astype(BF))
    tok = index.shape[0]
    sides = jnp.dot(jnp.concatenate(tables, 0), rows, preferred_element_type=F32)
    return jnp.concatenate([sides[:tok], sides[tok:]], 1)


def body(
    tokens,
    cotangent,
    norm_gain,
    router,
    dense_gate,
    dense_up,
    dense_down,
    expert_gate,
    expert_up,
    expert_down,
    routes,
):
    tok, width = tokens.shape
    experts = router.shape[1]
    cap = 5 * tok // (2 * experts)
    block = 2 * cap
    everything = experts * block

    values = tokens.astype(F32)
    inverse = lax.rsqrt(jnp.mean(values * values, -1, keepdims=True) + EPS)
    normed = (values * inverse * norm_gain).astype(BF)
    pair = jnp.concatenate([normed, cotangent], 0)

    routes_in = after(routes, pair)
    peer_routes = {k: receive_from(routes_in, k) for k in (1, 2, 3)}
    expert = weight_pieces(expert_gate[0], expert_up[0], expert_down[0])
    dense = weight_pieces(dense_gate, dense_up, dense_down)
    later = after(pair, *expert, *dense)
    peer = {k: receive_from(later if k != 2 else pair, k) for k in (2, 1, 3)}

    def to_experts(rows, index):
        places = jnp.concatenate([index, index + cap], 0)
        return over(pick_rows(picker(places, everything), rows))

    known = after(routes, *peer_routes.values())
    own_index = known * block + slots_of(known, experts)
    far_index = peer_routes[2] * block + slots_of(peer_routes[2], experts)
    own = to_experts(pair, own_index)
    far = to_experts(peer[2], far_index)
    chunk = everything // 2
    parts = [own[:chunk], own[chunk:]]
    near = [{k: receive_from(part, k) for k in (1, 3)} for part in parts]
    table = shuffle_table(cap, experts // 2)
    tables = (table, table.T)

    own_into, own_joint = hidden_grads([own], expert, tables)
    dense_part, unused = hidden_grads(
        [after(pair, own_into)] + [peer[k] for k in (1, 2, 3)], dense
    )
    near_into = [None, None]
    near_joint = [None, None]
    near_into[0], near_joint[0] = hidden_grads(
        [after(near[0][1], dense_part), near[0][3]], expert, tables
    )
    far_into, far_joint = hidden_grads([after(far, near_into[0])], expert, tables)
    far_back = over(far_into)
    near_into[1], near_joint[1] = hidden_grads(
        [after(near[1][1], far_into), near[1][3]], expert, tables
    )
    arrived = (near[1][1], near[1][3])
    near_back = []
    for i in (0, 1):
        first = after(near_into[i], *arrived) if i == 0 else near_into[i]
        near_back.append(send_to(first[:chunk], 1).astype(F32) + send_to(first[chunk:], 3).astype(F32))
    home1 = send_to(after(dense_part[tok : 2 * tok], near_into[1]), 1)
    home3 = send_to(after(dense_part[3 * tok :], near_into[1]), 3)

    joints = jnp.stack(
        [
            own_joint.reshape(experts, cap),
            jnp.concatenate([v[: chunk // 2] for v in near_joint]).reshape(experts, cap),
            far_joint.reshape(experts, cap),
            jnp.concatenate([v[chunk // 2 :] for v in near_joint]).reshape(experts, cap),
        ],
        1,
    )
    plane = lax.broadcasted_iota(jnp.int32, (1, PEERS, PEERS, 1), 1)
    offset = lax.broadcasted_iota(jnp.int32, (1, PEERS, PEERS, 1), 2)
    meant = plane == (lax.axis_index("y") + offset) % PEERS
    joints = jnp.sum(jnp.where(meant, joints[:, None], 0.0), 2).reshape(experts * PEERS, cap)
    joints = over(after(joints, far_back), ("ep", "y"))
    score = jnp.sum(joints.reshape(experts, PEERS, cap), 1)

    own_sum = own_into.astype(F32) + jnp.concatenate(near_back, 0)
    own_back = over(after(own_sum.astype(BF), joints))

    ids = lax.broadcasted_iota(jnp.int32, (1, 1, experts), 2)
    chosen = routes[..., None] == ids
    weights = router_weights(normed, router, chosen)
    far_weights = router_weights(peer[2][:tok], router, peer_routes[2][..., None] == ids)
    mixed = dense_part[2 * tok : 3 * tok].astype(F32)
    mixed = mixed + mix(far_index, far_weights, far_back, cap)
    home2 = send_to(mixed.astype(BF), 2)

    scores = jnp.sum(
        jnp.where(
            spread(routes * cap + own_index - routes * block, experts * cap),
            score.reshape(1, 1, -1),
            0.0,
        ),
        -1,
    )
    delta = weights[:, 0] * weights[:, 1] * (scores[:, 0] - scores[:, 1])
    signed = chosen[:, 0].astype(F32) - chosen[:, 1].astype(F32)
    grad_logits = signed * delta[:, None]
    local_router = lax.dot_general(
        grad_logits, normed.astype(F32), (((0,), (0,)), ((), ())), precision=HIGHEST
    )
    early = dense_part[:tok].astype(F32)
    early = early + jnp.dot(grad_logits, router.T, precision=HIGHEST)
    for piece in (home1, home3):
        early = early + piece.astype(F32)

    total = early + home2.astype(F32) + mix(own_index, weights, own_back, cap)
    local_gain = jnp.sum(total * values * inverse, 0, keepdims=True)
    axes = ("ep", "y", "core")
    devices = lax.axis_size(axes)
    local = jnp.concatenate([local_router, local_gain], 0).reshape(devices, -1)
    mine = jnp.sum(over(local, axes), 0, keepdims=True)
    sums = over(jnp.broadcast_to(mine, local.shape), axes).reshape(experts + 1, width)
    scaled = total * norm_gain
    mean_term = jnp.mean(scaled * values, -1, keepdims=True)
    input_grad = cotangent.astype(F32) + inverse * (
        scaled - values * inverse * inverse * mean_term
    )
    return (input_grad.astype(BF), sums[experts], sums[:experts].T)


def solution(mesh):
    ep, sp = mesh.devices.shape
    grid = Mesh(mesh.devices.reshape(ep, sp // 2, 2), ("ep", "y", "core"))
    shared = ("y", "core")
    rows = ("ep", "y", "core")
    return jax.shard_map(
        body,
        mesh=grid,
        in_specs=(
            P(rows, None),
            P(rows, None),
            P(),
            P(),
            P(None, shared),
            P(None, shared),
            P(shared, None),
            P("ep", None, shared),
            P("ep", None, shared),
            P("ep", shared, None),
            P(rows, None),
        ),
        out_specs=(P(rows, None), P(), P()),
        check_vma=False,
    )
```

```python
import jax
import jax.numpy as jnp
from jax import lax
from jax.experimental import pallas as pl
from jax.experimental.pallas import tpu as pltpu
from jax.sharding import Mesh, PartitionSpec as P

EPS = 1e-05
BF = jnp.bfloat16
F32 = jnp.float32
HIGHEST = lax.Precision.HIGHEST
PEERS = 4
VMEM_LIMIT = 50 * 1024 * 1024
TRANS = (((1,), (1,)), ((), ()))


def receive_from(value, k):
    return lax.ppermute(value, "y", [(i, (i - k) % PEERS) for i in range(PEERS)])


def send_to(value, k):
    return lax.ppermute(value, "y", [(i, (i + k) % PEERS) for i in range(PEERS)])


def swap(value):
    return lax.ppermute(value, "core", [(0, 1), (1, 0)])


def over(value, axes="ep"):
    return lax.all_to_all(value, axes, split_axis=0, concat_axis=0, tiled=True)


def after(value, *others):
    return lax.optimization_barrier((value,) + others)[0]


def weight_pieces(gate, up, down):
    return [lax.all_gather(v, "core", axis=0, tiled=True) for v in (gate.T, up.T, down)]


def shuffle_table(cap, group):
    size = 2 * group * cap
    row = lax.broadcasted_iota(jnp.int32, (size, size), 0)
    col = lax.broadcasted_iota(jnp.int32, (size, size), 1)
    part, left = row // (group * cap), row % (group * cap)
    return (col == left // cap * (2 * cap) + part * cap + left % cap).astype(BF)


def hidden_kernel(count, mixed, *refs):
    sources = refs[:count]
    pieces = refs[count : count + 3]
    refs = refs[count + 3 :]
    if mixed:
        table, table_back = refs[:2]
        refs = refs[2:]
    into, joint, weights, normed, other, both, back, grads, sems = refs
    step = pl.program_id(0)
    part, width = pieces[0].shape
    half = weights.shape[0] // 3
    copies = [
        pltpu.make_async_copy(pieces[i], weights.at[pl.ds(i * half, part), :], sems.at[i])
        for i in range(3)
    ]

    @pl.when(step == 0)
    def _():
        for copy in copies[2:] + copies[:2]:
            copy.start()
        if half > part:
            for i in range(3):
                weights[i * half + part : (i + 1) * half, :] = jnp.zeros((half - part, width), BF)

    size = sources[0].shape[0] // 2
    each = normed.shape[0] // size
    for p in range(count):

        @pl.when(step == p // each)
        def _(p=p):
            first = p % each * size
            if mixed:
                chunk = table.shape[0]
                for i in range(2 * size // chunk):
                    got = jnp.dot(
                        table[...],
                        sources[p][i * chunk : (i + 1) * chunk, :],
                        preferred_element_type=F32,
                    ).astype(BF)
                    at = slice(first + i * chunk // 2, first + (i + 1) * chunk // 2)
                    normed[at, :] = got[: chunk // 2]
                    other[at, :] = got[chunk // 2 :]
            else:
                at = slice(first, first + size)
                normed[at, :] = sources[p][:size, :]
                other[at, :] = sources[p][size:, :]

    def wait(i, j):
        @pl.when(step == 0)
        def _():
            for copy in copies[i:j]:
                copy.wait()

    wait(2, 3)
    back[...] = lax.dot_general(
        other[...], weights[2 * half :, :], TRANS, preferred_element_type=F32
    )
    wait(0, 2)
    both[...] = lax.dot_general(
        normed[...], weights[: 2 * half, :], TRANS, preferred_element_type=F32
    )
    gate, up, dy = both[:, :half], both[:, half:], back[...]
    sig = jax.nn.sigmoid(gate)
    active = gate * sig
    grad_up = dy * active
    grads[:, half:] = grad_up.astype(BF)
    grads[:, :half] = (dy * up * (sig + active * (1.0 - sig))).astype(BF)
    score = jnp.sum(grad_up * up, -1, keepdims=True)
    joint[...] = jnp.broadcast_to(score, joint.shape)
    if mixed:
        other[...] = jnp.dot(
            grads[...], weights[: 2 * half, :], preferred_element_type=F32
        ).astype(BF)
        chunk = table.shape[0]
        for i in range(2 * normed.shape[0] // chunk):
            at = slice(i * chunk // 2, (i + 1) * chunk // 2)
            sides = jnp.concatenate([other[at, : width // 2], other[at, width // 2 :]], 0)
            into[i * chunk : (i + 1) * chunk, :] = jnp.dot(
                table_back[...], sides, preferred_element_type=F32
            ).astype(BF)
    else:
        into[...] = jnp.dot(
            grads[...], weights[: 2 * half, :], preferred_element_type=F32
        ).astype(BF)


def hidden_grads(sources, pieces, tables=()):
    count = len(sources)
    mixed = len(tables) > 0
    size = sources[0].shape[0] // 2
    part, width = pieces[0].shape
    half = -(-part // 128) * 128
    total = count * size
    step_rows = min(total, 320) if mixed else 2 * size
    out = (2 * total, width // 2) if mixed else (total, width)
    block = (2 * step_rows, width // 2) if mixed else (step_rows, width)

    def whole(value):
        return pl.BlockSpec(value.shape, lambda i: (0, 0), pipeline_mode=pl.Buffered(1))

    into, joint = pl.pallas_call(
        lambda *refs: hidden_kernel(count, mixed, *refs),
        grid=(total // step_rows,),
        in_specs=[whole(v) for v in sources]
        + [pl.BlockSpec(memory_space=pl.ANY)] * 3
        + [whole(v) for v in tables],
        out_specs=[
            pl.BlockSpec(block, lambda i: (i, 0)),
            pl.BlockSpec((step_rows, 128), lambda i: (i, 0)),
        ],
        out_shape=[jax.ShapeDtypeStruct(out, BF), jax.ShapeDtypeStruct((total, 128), F32)],
        scratch_shapes=[
            pltpu.VMEM((3 * half, width), BF),
            pltpu.VMEM((step_rows, width), BF),
            pltpu.VMEM((step_rows, width), BF),
            pltpu.VMEM((step_rows, 2 * half), F32),
            pltpu.VMEM((step_rows, half), F32),
            pltpu.VMEM((step_rows, 2 * half), BF),
            pltpu.SemaphoreType.DMA((3,)),
        ],
        compiler_params=pltpu.CompilerParams(vmem_limit_bytes=VMEM_LIMIT),
        cost_estimate=pl.CostEstimate(
            flops=10 * total * width * half,
            bytes_accessed=6 * half * width + 6 * total * width,
            transcendentals=total * half,
        ),
    )(*sources, *pieces, *tables)
    return into, joint[:, 0]


def pick_kernel(table, rows, out):
    out[...] = jnp.dot(table[...], rows[...], preferred_element_type=F32).astype(BF)


def pick_rows(table, source):
    rows, depth = table.shape
    width = source.shape[1]
    block = 512 if width % 512 == 0 else 128
    return pl.pallas_call(
        pick_kernel,
        grid=(width // block,),
        in_specs=[
            pl.BlockSpec((rows, depth), lambda i: (0, 0)),
            pl.BlockSpec((depth, block), lambda i: (0, i)),
        ],
        out_specs=pl.BlockSpec((rows, block), lambda i: (0, i)),
        out_shape=jax.ShapeDtypeStruct((rows, width), BF),
        compiler_params=pltpu.CompilerParams(vmem_limit_bytes=VMEM_LIMIT),
        cost_estimate=pl.CostEstimate(
            flops=2 * rows * depth * width,
            bytes_accessed=2 * width * (rows + depth),
            transcendentals=0,
        ),
    )(table, source)


def slots_of(routes, experts):
    tok = routes.shape[0]
    flat = routes.reshape(2 * tok, 1)
    hits = (flat == lax.broadcasted_iota(jnp.int32, (1, experts), 1)).astype(BF)
    place = lax.broadcasted_iota(jnp.int32, (2 * tok, 2 * tok), 0)
    before = (lax.broadcasted_iota(jnp.int32, (2 * tok, 2 * tok), 1) < place).astype(BF)
    places = jnp.dot(before, hits, preferred_element_type=F32)
    return jnp.sum(hits.astype(F32) * places, -1).astype(jnp.int32).reshape(tok, 2)


def spread(index, rows):
    return index[..., None] == lax.broadcasted_iota(jnp.int32, (1, 1, rows), 2)


def picker(index, rows):
    hits = lax.broadcasted_iota(jnp.int32, (rows, 1), 0)
    return (hits == index[:, 0][None]).astype(BF) + (hits == index[:, 1][None]).astype(BF)


def router_weights(normed, router, chosen):
    logits = jnp.dot(normed.astype(F32), router, precision=HIGHEST)
    picked = jnp.sum(jnp.where(chosen, logits[:, None, :], 0.0), -1)
    one = jax.nn.sigmoid(picked[:, 0:1] - picked[:, 1:2])
    return jnp.concatenate([one, 1.0 - one], 1)


def mix(index, weights, rows, cap):
    count = rows.shape[0]
    tables = []
    for shift in (0, cap):
        hot = spread(index + shift, count)
        tables.append(jnp.sum(jnp.where(hot, weights[..., None], 0.0), 1).astype(BF))
    tok = index.shape[0]
    sides = jnp.dot(jnp.concatenate(tables, 0), rows, preferred_element_type=F32)
    return jnp.concatenate([sides[:tok], sides[tok:]], 1)


def body(
    tokens,
    cotangent,
    norm_gain,
    router,
    dense_gate,
    dense_up,
    dense_down,
    expert_gate,
    expert_up,
    expert_down,
    routes,
):
    tok, width = tokens.shape
    experts = router.shape[1]
    cap = 5 * tok // (2 * experts)
    block = 2 * cap
    everything = experts * block

    values = tokens.astype(F32)
    inverse = lax.rsqrt(jnp.mean(values * values, -1, keepdims=True) + EPS)
    normed = (values * inverse * norm_gain).astype(BF)
    pair = jnp.concatenate([normed, cotangent], 0)

    routes_in = after(routes, pair)
    peer_routes = {k: receive_from(routes_in, k) for k in (1, 2, 3)}
    expert = weight_pieces(expert_gate[0], expert_up[0], expert_down[0])
    dense = weight_pieces(dense_gate, dense_up, dense_down)
    peer = {k: receive_from(pair, k) for k in (2, 1, 3)}

    def to_experts(rows, index):
        places = jnp.concatenate([index, index + cap], 0)
        return over(pick_rows(picker(places, everything), rows))

    known = after(routes, *peer_routes.values())
    own_index = known * block + slots_of(known, experts)
    far_index = peer_routes[2] * block + slots_of(peer_routes[2], experts)
    own = to_experts(pair, own_index)
    far = to_experts(peer[2], far_index)
    chunk = everything // 2
    parts = [own[:chunk], own[chunk:]]
    near = [{k: receive_from(part, k) for k in (1, 3)} for part in parts]
    table = shuffle_table(cap, experts // 2)
    tables = (table, table.T)

    own_into, own_joint = hidden_grads([own], expert, tables)
    dense_part, unused = hidden_grads(
        [after(pair, own_into)] + [peer[k] for k in (1, 2, 3)], dense
    )
    far_into, far_joint = hidden_grads([after(far, dense_part)], expert, tables)
    far_back = over(far_into)
    near_into = [None, None]
    near_joint = [None, None]
    near_into[0], near_joint[0] = hidden_grads(
        [after(near[0][1], far_into), near[0][3]], expert, tables
    )
    near_into[1], near_joint[1] = hidden_grads(
        [after(near[1][1], near_into[0]), near[1][3]], expert, tables
    )
    near_into[1] = after(near_into[1], far_back)
    arrived = (near[1][1], near[1][3])
    near_back = []
    for i in (0, 1):
        first = after(near_into[i], *arrived) if i == 0 else near_into[i]
        near_back.append(send_to(first[:chunk], 1).astype(F32) + send_to(first[chunk:], 3).astype(F32))
    home1 = send_to(after(dense_part[tok : 2 * tok], near_into[1]), 1)
    home3 = send_to(after(dense_part[3 * tok :], near_into[1]), 3)

    joints = jnp.stack(
        [
            own_joint.reshape(experts, cap),
            jnp.concatenate([v[: chunk // 2] for v in near_joint]).reshape(experts, cap),
            far_joint.reshape(experts, cap),
            jnp.concatenate([v[chunk // 2 :] for v in near_joint]).reshape(experts, cap),
        ],
        1,
    )
    plane = lax.broadcasted_iota(jnp.int32, (1, PEERS, PEERS, 1), 1)
    offset = lax.broadcasted_iota(jnp.int32, (1, PEERS, PEERS, 1), 2)
    meant = plane == (lax.axis_index("y") + offset) % PEERS
    joints = jnp.sum(jnp.where(meant, joints[:, None], 0.0), 2).reshape(experts * PEERS, cap)
    joints = over(after(joints, far_back), ("ep", "y"))
    score = jnp.sum(joints.reshape(experts, PEERS, cap), 1)

    own_sum = own_into.astype(F32) + jnp.concatenate(near_back, 0)
    own_back = over(after(own_sum.astype(BF), joints))

    ids = lax.broadcasted_iota(jnp.int32, (1, 1, experts), 2)
    chosen = routes[..., None] == ids
    weights = router_weights(normed, router, chosen)
    far_weights = router_weights(peer[2][:tok], router, peer_routes[2][..., None] == ids)
    mixed = dense_part[2 * tok : 3 * tok].astype(F32)
    mixed = mixed + mix(far_index, far_weights, far_back, cap)
    home2 = send_to(mixed.astype(BF), 2)

    scores = jnp.sum(
        jnp.where(
            spread(routes * cap + own_index - routes * block, experts * cap),
            score.reshape(1, 1, -1),
            0.0,
        ),
        -1,
    )
    delta = weights[:, 0] * weights[:, 1] * (scores[:, 0] - scores[:, 1])
    signed = chosen[:, 0].astype(F32) - chosen[:, 1].astype(F32)
    grad_logits = signed * delta[:, None]
    local_router = lax.dot_general(
        grad_logits, normed.astype(F32), (((0,), (0,)), ((), ())), precision=HIGHEST
    )
    early = dense_part[:tok].astype(F32)
    early = early + jnp.dot(grad_logits, router.T, precision=HIGHEST)
    for piece in (home1, home3):
        early = early + piece.astype(F32)

    total = early + home2.astype(F32) + mix(own_index, weights, own_back, cap)
    local_gain = jnp.sum(total * values * inverse, 0, keepdims=True)
    axes = ("ep", "y", "core")
    devices = lax.axis_size(axes)
    local = jnp.concatenate([local_router, local_gain], 0).reshape(devices, -1)
    mine = jnp.sum(over(local, axes), 0, keepdims=True)
    sums = over(jnp.broadcast_to(mine, local.shape), axes).reshape(experts + 1, width)
    scaled = total * norm_gain
    mean_term = jnp.mean(scaled * values, -1, keepdims=True)
    input_grad = cotangent.astype(F32) + inverse * (
        scaled - values * inverse * inverse * mean_term
    )
    return (input_grad.astype(BF), sums[experts], sums[:experts].T)


def solution(mesh):
    ep, sp = mesh.devices.shape
    grid = Mesh(mesh.devices.reshape(ep, sp // 2, 2), ("ep", "y", "core"))
    shared = ("y", "core")
    rows = ("ep", "y", "core")
    return jax.shard_map(
        body,
        mesh=grid,
        in_specs=(
            P(rows, None),
            P(rows, None),
            P(),
            P(),
            P(None, shared),
            P(None, shared),
            P(shared, None),
            P("ep", None, shared),
            P("ep", None, shared),
            P("ep", shared, None),
            P(rows, None),
        ),
        out_specs=(P(rows, None), P(), P()),
        check_vma=False,
    )
```

```python
import jax
import jax.numpy as jnp
from jax import lax
from jax.experimental import pallas as pl
from jax.experimental.pallas import tpu as pltpu
from jax.sharding import Mesh, PartitionSpec as P

EPS = 1e-05
BF = jnp.bfloat16
F32 = jnp.float32
HIGHEST = lax.Precision.HIGHEST
PEERS = 4
VMEM_LIMIT = 50 * 1024 * 1024
TRANS = (((1,), (1,)), ((), ()))


def receive_from(value, k):
    return lax.ppermute(value, "y", [(i, (i - k) % PEERS) for i in range(PEERS)])


def send_to(value, k):
    return lax.ppermute(value, "y", [(i, (i + k) % PEERS) for i in range(PEERS)])


def swap(value):
    return lax.ppermute(value, "core", [(0, 1), (1, 0)])


def over(value, axes="ep"):
    return lax.all_to_all(value, axes, split_axis=0, concat_axis=0, tiled=True)


def after(value, *others):
    return lax.optimization_barrier((value,) + others)[0]


def weight_pieces(gate, up, down):
    both = [gate.T, up.T, down]
    return [piece for value in both for piece in (value, swap(value))]


def shuffle_table(cap, group):
    size = 2 * group * cap
    row = lax.broadcasted_iota(jnp.int32, (size, size), 0)
    col = lax.broadcasted_iota(jnp.int32, (size, size), 1)
    part, left = row // (group * cap), row % (group * cap)
    return (col == left // cap * (2 * cap) + part * cap + left % cap).astype(BF)


def hidden_kernel(lengths, mixed, *refs):
    count = sum(lengths)
    taken, sources = 0, []
    for length in lengths:
        sources.append(refs[taken : taken + length])
        taken += length
    pieces = refs[count : count + 6]
    refs = refs[count + 6 :]
    if mixed:
        table, table_back = refs[:2]
        refs = refs[2:]
    into, joint, weights, normed, other, both, back, grads, sems = refs
    step = pl.program_id(0)
    part, width = pieces[0].shape
    half = weights.shape[0] // 3
    copies = []
    for i in range(6):
        start = i // 2 * half + i % 2 * part
        copies.append(
            pltpu.make_async_copy(pieces[i], weights.at[pl.ds(start, part), :], sems.at[i])
        )

    @pl.when(step == 0)
    def _():
        for copy in copies[4:] + copies[:4]:
            copy.start()
        if half > 2 * part:
            for i in range(3):
                weights[i * half + 2 * part : (i + 1) * half, :] = jnp.zeros(
                    (half - 2 * part, width), BF
                )

    size = sources[0][0].shape[0] // 2
    each = normed.shape[0] // size
    for p in range(len(lengths)):

        @pl.when(step == p // each)
        def _(p=p):
            first = p % each * size
            if mixed:
                chunk = table.shape[0]
                for i in range(2 * size // chunk):
                    got = jnp.dot(
                        table[...],
                        sources[p][0][i * chunk : (i + 1) * chunk, :],
                        preferred_element_type=F32,
                    ).astype(BF)
                    at = slice(first + i * chunk // 2, first + (i + 1) * chunk // 2)
                    normed[at, :] = got[: chunk // 2]
                    other[at, :] = got[chunk // 2 :]
            else:
                at = slice(first, first + size)
                if lengths[p] == 1:
                    normed[at, :] = sources[p][0][:size, :]
                    other[at, :] = sources[p][0][size:, :]
                else:
                    normed[at, :] = sources[p][0][...]
                    other[at, :] = sources[p][1][...]

    def wait(i, j):
        @pl.when(step == 0)
        def _():
            for copy in copies[i:j]:
                copy.wait()

    wait(4, 6)
    back[...] = lax.dot_general(
        other[...], weights[2 * half :, :], TRANS, preferred_element_type=F32
    )
    wait(0, 4)
    both[...] = lax.dot_general(
        normed[...], weights[: 2 * half, :], TRANS, preferred_element_type=F32
    )
    gate, up, dy = both[:, :half], both[:, half:], back[...]
    sig = jax.nn.sigmoid(gate)
    active = gate * sig
    grad_up = dy * active
    grads[:, half:] = grad_up.astype(BF)
    grads[:, :half] = (dy * up * (sig + active * (1.0 - sig))).astype(BF)
    score = jnp.sum(grad_up * up, -1, keepdims=True)
    joint[...] = jnp.broadcast_to(score, joint.shape)
    if mixed:
        other[...] = jnp.dot(
            grads[...], weights[: 2 * half, :], preferred_element_type=F32
        ).astype(BF)
        chunk = table.shape[0]
        for i in range(2 * normed.shape[0] // chunk):
            at = slice(i * chunk // 2, (i + 1) * chunk // 2)
            sides = jnp.concatenate([other[at, : width // 2], other[at, width // 2 :]], 0)
            into[i * chunk : (i + 1) * chunk, :] = jnp.dot(
                table_back[...], sides, preferred_element_type=F32
            ).astype(BF)
    else:
        into[...] = jnp.dot(
            grads[...], weights[: 2 * half, :], preferred_element_type=F32
        ).astype(BF)


def hidden_grads(sources, pieces, tables=()):
    count = len(sources)
    lengths = [len(v) for v in sources]
    mixed = len(tables) > 0
    size = sources[0][0].shape[0] // 2
    sources = [v for source in sources for v in source]
    part, width = pieces[0].shape
    half = -(-2 * part // 128) * 128
    total = count * size
    step_rows = min(total, 320) if mixed else 2 * size
    out = (2 * total, width // 2) if mixed else (total, width)
    block = (2 * step_rows, width // 2) if mixed else (step_rows, width)

    def whole(value):
        return pl.BlockSpec(value.shape, lambda i: (0, 0), pipeline_mode=pl.Buffered(1))

    into, joint = pl.pallas_call(
        lambda *refs: hidden_kernel(lengths, mixed, *refs),
        grid=(total // step_rows,),
        in_specs=[whole(v) for v in sources]
        + [pl.BlockSpec(memory_space=pl.ANY)] * 6
        + [whole(v) for v in tables],
        out_specs=[
            pl.BlockSpec(block, lambda i: (i, 0)),
            pl.BlockSpec((step_rows, 128), lambda i: (i, 0)),
        ],
        out_shape=[jax.ShapeDtypeStruct(out, BF), jax.ShapeDtypeStruct((total, 128), F32)],
        scratch_shapes=[
            pltpu.VMEM((3 * half, width), BF),
            pltpu.VMEM((step_rows, width), BF),
            pltpu.VMEM((step_rows, width), BF),
            pltpu.VMEM((step_rows, 2 * half), F32),
            pltpu.VMEM((step_rows, half), F32),
            pltpu.VMEM((step_rows, 2 * half), BF),
            pltpu.SemaphoreType.DMA((6,)),
        ],
        compiler_params=pltpu.CompilerParams(vmem_limit_bytes=VMEM_LIMIT),
        cost_estimate=pl.CostEstimate(
            flops=10 * total * width * half,
            bytes_accessed=6 * half * width + 6 * total * width,
            transcendentals=total * half,
        ),
    )(*sources, *pieces, *tables)
    return into, joint[:, 0]


def pick_kernel(table, rows, out):
    out[...] = jnp.dot(table[...], rows[...], preferred_element_type=F32).astype(BF)


def pick_rows(table, source):
    rows, depth = table.shape
    width = source.shape[1]
    block = 512 if width % 512 == 0 else 128
    return pl.pallas_call(
        pick_kernel,
        grid=(width // block,),
        in_specs=[
            pl.BlockSpec((rows, depth), lambda i: (0, 0)),
            pl.BlockSpec((depth, block), lambda i: (0, i)),
        ],
        out_specs=pl.BlockSpec((rows, block), lambda i: (0, i)),
        out_shape=jax.ShapeDtypeStruct((rows, width), BF),
        compiler_params=pltpu.CompilerParams(vmem_limit_bytes=VMEM_LIMIT),
        cost_estimate=pl.CostEstimate(
            flops=2 * rows * depth * width,
            bytes_accessed=2 * width * (rows + depth),
            transcendentals=0,
        ),
    )(table, source)


def slots_of(routes, experts):
    tok = routes.shape[0]
    flat = routes.reshape(2 * tok, 1)
    hits = (flat == lax.broadcasted_iota(jnp.int32, (1, experts), 1)).astype(BF)
    place = lax.broadcasted_iota(jnp.int32, (2 * tok, 2 * tok), 0)
    before = (lax.broadcasted_iota(jnp.int32, (2 * tok, 2 * tok), 1) < place).astype(BF)
    places = jnp.dot(before, hits, preferred_element_type=F32)
    return jnp.sum(hits.astype(F32) * places, -1).astype(jnp.int32).reshape(tok, 2)


def spread(index, rows):
    return index[..., None] == lax.broadcasted_iota(jnp.int32, (1, 1, rows), 2)


def picker(index, rows):
    hits = lax.broadcasted_iota(jnp.int32, (rows, 1), 0)
    return (hits == index[:, 0][None]).astype(BF) + (hits == index[:, 1][None]).astype(BF)


def router_weights(normed, router, chosen):
    logits = jnp.dot(normed.astype(F32), router, precision=HIGHEST)
    picked = jnp.sum(jnp.where(chosen, logits[:, None, :], 0.0), -1)
    one = jax.nn.sigmoid(picked[:, 0:1] - picked[:, 1:2])
    return jnp.concatenate([one, 1.0 - one], 1)


def mix(index, weights, rows, cap):
    count = rows.shape[0]
    tables = []
    for shift in (0, cap):
        hot = spread(index + shift, count)
        tables.append(jnp.sum(jnp.where(hot, weights[..., None], 0.0), 1).astype(BF))
    tok = index.shape[0]
    sides = jnp.dot(jnp.concatenate(tables, 0), rows, preferred_element_type=F32)
    return jnp.concatenate([sides[:tok], sides[tok:]], 1)


def body(
    tokens,
    cotangent,
    norm_gain,
    router,
    dense_gate,
    dense_up,
    dense_down,
    expert_gate,
    expert_up,
    expert_down,
    routes,
):
    tok, width = tokens.shape
    experts = router.shape[1]
    cap = 5 * tok // (2 * experts)
    block = 2 * cap
    everything = experts * block

    values = tokens.astype(F32)
    inverse = lax.rsqrt(jnp.mean(values * values, -1, keepdims=True) + EPS)
    normed = (values * inverse * norm_gain).astype(BF)
    pair = jnp.concatenate([normed, cotangent], 0)

    peer_cot = {k: receive_from(cotangent, k) for k in (1, 3)}
    expert = weight_pieces(expert_gate[0], expert_up[0], expert_down[0])
    far_routes = receive_from(routes, 2)

    def pick_for(rows, index):
        places = jnp.concatenate([index, index + cap], 0)
        return pick_rows(picker(places, everything), rows)

    own_index = routes * block + slots_of(routes, experts)
    far_index = far_routes * block + slots_of(far_routes, experts)
    ready = tuple(peer_cot.values()) + tuple(expert[1::2]) + (far_routes,)
    own_send = after(pick_for(pair, own_index), *ready)
    own = over(own_send)
    far_pair = receive_from(pair, 2)
    peer_normed = {k: receive_from(normed, k) for k in (1, 3)}
    dense = weight_pieces(*(after(v, own_send) for v in (dense_gate, dense_up, dense_down)))
    far = over(pick_for(after(far_pair, *dense[1::2]), far_index))
    chunk = everything // 2
    parts = [own[:chunk], own[chunk:]]
    near = [{k: receive_from(part, k) for k in (1, 3)} for part in parts]
    table = shuffle_table(cap, experts // 2)
    tables = (table, table.T)

    own_into, own_joint = hidden_grads([(own,)], expert, tables)
    dense_part, unused = hidden_grads(
        [
            (after(pair, own_into),),
            (peer_normed[1], peer_cot[1]),
            (far_pair,),
            (peer_normed[3], peer_cot[3]),
        ],
        dense,
    )
    far_into, far_joint = hidden_grads([(after(far, dense_part),)], expert, tables)
    far_back = over(far_into)
    near_into = [None, None]
    near_joint = [None, None]
    near_into[0], near_joint[0] = hidden_grads(
        [(after(near[0][1], far_into),), (near[0][3],)], expert, tables
    )
    near_into[1], near_joint[1] = hidden_grads(
        [(after(near[1][1], near_into[0]),), (near[1][3],)], expert, tables
    )
    near_into[1] = after(near_into[1], far_back)
    arrived = (near[1][1], near[1][3])
    near_back = []
    for i in (0, 1):
        first = after(near_into[i], *arrived) if i == 0 else near_into[i]
        near_back.append(send_to(first[:chunk], 1).astype(F32) + send_to(first[chunk:], 3).astype(F32))
    home1 = send_to(after(dense_part[tok : 2 * tok], near_back[1]), 1)
    home3 = send_to(after(dense_part[3 * tok :], near_back[1]), 3)

    joints = jnp.stack(
        [
            own_joint.reshape(experts, cap),
            jnp.concatenate([v[: chunk // 2] for v in near_joint]).reshape(experts, cap),
            far_joint.reshape(experts, cap),
            jnp.concatenate([v[chunk // 2 :] for v in near_joint]).reshape(experts, cap),
        ],
        1,
    )
    joints = over(after(joints.reshape(experts, PEERS * cap), far_back))
    joints = joints.reshape(experts, PEERS, cap)
    shares = [send_to(joints[:, k], k) for k in (1, 2, 3)]

    own_sum = own_into.astype(F32) + jnp.concatenate(near_back, 0)
    own_sum = after(own_sum.astype(BF), joints)
    own_back = over(own_sum)
    score = after(joints[:, 0], own_sum)
    for share in shares:
        score = score + share

    ids = lax.broadcasted_iota(jnp.int32, (1, 1, experts), 2)
    chosen = routes[..., None] == ids
    weights = router_weights(normed, router, chosen)
    far_weights = router_weights(far_pair[:tok], router, far_routes[..., None] == ids)
    mixed = dense_part[2 * tok : 3 * tok].astype(F32)
    mixed = mixed + mix(far_index, far_weights, far_back, cap)
    home2 = send_to(mixed.astype(BF), 2)

    scores = jnp.sum(
        jnp.where(
            spread(routes * cap + own_index - routes * block, experts * cap),
            score.reshape(1, 1, -1),
            0.0,
        ),
        -1,
    )
    delta = weights[:, 0] * weights[:, 1] * (scores[:, 0] - scores[:, 1])
    signed = chosen[:, 0].astype(F32) - chosen[:, 1].astype(F32)
    grad_logits = signed * delta[:, None]
    local_router = lax.dot_general(
        grad_logits, normed.astype(F32), (((0,), (0,)), ((), ())), precision=HIGHEST
    )
    early = dense_part[:tok].astype(F32)
    early = early + jnp.dot(grad_logits, router.T, precision=HIGHEST)
    for piece in (home1, home3):
        early = early + piece.astype(F32)

    total = early + home2.astype(F32) + mix(own_index, weights, own_back, cap)
    local_gain = jnp.sum(total * values * inverse, 0, keepdims=True)
    axes = ("ep", "y", "core")
    devices = lax.axis_size(axes)
    local = jnp.concatenate([local_router, local_gain], 0).reshape(devices, -1)
    mine = jnp.sum(over(local, axes), 0, keepdims=True)
    sums = over(jnp.broadcast_to(mine, local.shape), axes).reshape(experts + 1, width)
    scaled = total * norm_gain
    mean_term = jnp.mean(scaled * values, -1, keepdims=True)
    input_grad = cotangent.astype(F32) + inverse * (
        scaled - values * inverse * inverse * mean_term
    )
    return (input_grad.astype(BF), sums[experts], sums[:experts].T)


def solution(mesh):
    ep, sp = mesh.devices.shape
    grid = Mesh(mesh.devices.reshape(ep, sp // 2, 2), ("ep", "y", "core"))
    shared = ("y", "core")
    rows = ("ep", "y", "core")
    return jax.shard_map(
        body,
        mesh=grid,
        in_specs=(
            P(rows, None),
            P(rows, None),
            P(),
            P(),
            P(None, shared),
            P(None, shared),
            P(shared, None),
            P("ep", None, shared),
            P("ep", None, shared),
            P("ep", shared, None),
            P(rows, None),
        ),
        out_specs=(P(rows, None), P(), P()),
        check_vma=False,
    )
```

```python
import jax
import jax.numpy as jnp
from jax import lax
from jax.experimental import pallas as pl
from jax.experimental.pallas import tpu as pltpu
from jax.sharding import Mesh, PartitionSpec as P

EPS = 1e-05
BF = jnp.bfloat16
F32 = jnp.float32
HIGHEST = lax.Precision.HIGHEST
PEERS = 4
VMEM_LIMIT = 50 * 1024 * 1024
TRANS = (((1,), (1,)), ((), ()))


def receive_from(value, k):
    return lax.ppermute(value, "y", [(i, (i - k) % PEERS) for i in range(PEERS)])


def send_to(value, k):
    return lax.ppermute(value, "y", [(i, (i + k) % PEERS) for i in range(PEERS)])


def swap(value):
    return lax.ppermute(value, "core", [(0, 1), (1, 0)])


def over(value, axes="ep"):
    return lax.all_to_all(value, axes, split_axis=0, concat_axis=0, tiled=True)


def after(value, *others):
    return lax.optimization_barrier((value,) + others)[0]


def weight_pieces(gate, up, down):
    both = [gate.T, up.T, down]
    return [piece for value in both for piece in (value, swap(value))]


def shuffle_table(cap, group):
    size = 2 * group * cap
    row = lax.broadcasted_iota(jnp.int32, (size, size), 0)
    col = lax.broadcasted_iota(jnp.int32, (size, size), 1)
    part, left = row // (group * cap), row % (group * cap)
    return (col == left // cap * (2 * cap) + part * cap + left % cap).astype(BF)


def hidden_kernel(lengths, mixed, *refs):
    count = sum(lengths)
    taken, sources = 0, []
    for length in lengths:
        sources.append(refs[taken : taken + length])
        taken += length
    pieces = refs[count : count + 6]
    refs = refs[count + 6 :]
    if mixed:
        table, table_back = refs[:2]
        refs = refs[2:]
    into, joint, weights, normed, other, both, back, grads, sems = refs
    step = pl.program_id(0)
    part, width = pieces[0].shape
    half = weights.shape[0] // 3
    copies = []
    for i in range(6):
        start = i // 2 * half + i % 2 * part
        copies.append(
            pltpu.make_async_copy(pieces[i], weights.at[pl.ds(start, part), :], sems.at[i])
        )

    @pl.when(step == 0)
    def _():
        for copy in copies[4:] + copies[:4]:
            copy.start()
        if half > 2 * part:
            for i in range(3):
                weights[i * half + 2 * part : (i + 1) * half, :] = jnp.zeros(
                    (half - 2 * part, width), BF
                )

    size = sources[0][0].shape[0] // 2
    each = normed.shape[0] // size
    for p in range(len(lengths)):

        @pl.when(step == p // each)
        def _(p=p):
            first = p % each * size
            if mixed:
                chunk = table.shape[0]
                for i in range(2 * size // chunk):
                    got = jnp.dot(
                        table[...],
                        sources[p][0][i * chunk : (i + 1) * chunk, :],
                        preferred_element_type=F32,
                    ).astype(BF)
                    at = slice(first + i * chunk // 2, first + (i + 1) * chunk // 2)
                    normed[at, :] = got[: chunk // 2]
                    other[at, :] = got[chunk // 2 :]
            else:
                at = slice(first, first + size)
                if lengths[p] == 1:
                    normed[at, :] = sources[p][0][:size, :]
                    other[at, :] = sources[p][0][size:, :]
                else:
                    head, rest = sources[p]
                    early = head.shape[0]
                    late = size - early
                    normed[at, :] = rest[late:, :]
                    other[first : first + early, :] = head[...]
                    other[first + early : first + size, :] = rest[:late, :]

    def wait(i, j):
        @pl.when(step == 0)
        def _():
            for copy in copies[i:j]:
                copy.wait()

    wait(4, 6)
    back[...] = lax.dot_general(
        other[...], weights[2 * half :, :], TRANS, preferred_element_type=F32
    )
    wait(0, 4)
    both[...] = lax.dot_general(
        normed[...], weights[: 2 * half, :], TRANS, preferred_element_type=F32
    )
    gate, up, dy = both[:, :half], both[:, half:], back[...]
    sig = jax.nn.sigmoid(gate)
    active = gate * sig
    grad_up = dy * active
    grads[:, half:] = grad_up.astype(BF)
    grads[:, :half] = (dy * up * (sig + active * (1.0 - sig))).astype(BF)
    score = jnp.sum(grad_up * up, -1, keepdims=True)
    joint[...] = jnp.broadcast_to(score, joint.shape)
    if mixed:
        other[...] = jnp.dot(
            grads[...], weights[: 2 * half, :], preferred_element_type=F32
        ).astype(BF)
        chunk = table.shape[0]
        for i in range(2 * normed.shape[0] // chunk):
            at = slice(i * chunk // 2, (i + 1) * chunk // 2)
            sides = jnp.concatenate([other[at, : width // 2], other[at, width // 2 :]], 0)
            into[i * chunk : (i + 1) * chunk, :] = jnp.dot(
                table_back[...], sides, preferred_element_type=F32
            ).astype(BF)
    else:
        into[...] = jnp.dot(
            grads[...], weights[: 2 * half, :], preferred_element_type=F32
        ).astype(BF)


def hidden_grads(sources, pieces, tables=()):
    count = len(sources)
    lengths = [len(v) for v in sources]
    mixed = len(tables) > 0
    size = sources[0][0].shape[0] // 2
    sources = [v for source in sources for v in source]
    part, width = pieces[0].shape
    half = -(-2 * part // 128) * 128
    total = count * size
    step_rows = min(total, 320) if mixed else 2 * size
    out = (2 * total, width // 2) if mixed else (total, width)
    block = (2 * step_rows, width // 2) if mixed else (step_rows, width)

    def whole(value):
        return pl.BlockSpec(value.shape, lambda i: (0, 0), pipeline_mode=pl.Buffered(1))

    into, joint = pl.pallas_call(
        lambda *refs: hidden_kernel(lengths, mixed, *refs),
        grid=(total // step_rows,),
        in_specs=[whole(v) for v in sources]
        + [pl.BlockSpec(memory_space=pl.ANY)] * 6
        + [whole(v) for v in tables],
        out_specs=[
            pl.BlockSpec(block, lambda i: (i, 0)),
            pl.BlockSpec((step_rows, 128), lambda i: (i, 0)),
        ],
        out_shape=[jax.ShapeDtypeStruct(out, BF), jax.ShapeDtypeStruct((total, 128), F32)],
        scratch_shapes=[
            pltpu.VMEM((3 * half, width), BF),
            pltpu.VMEM((step_rows, width), BF),
            pltpu.VMEM((step_rows, width), BF),
            pltpu.VMEM((step_rows, 2 * half), F32),
            pltpu.VMEM((step_rows, half), F32),
            pltpu.VMEM((step_rows, 2 * half), BF),
            pltpu.SemaphoreType.DMA((6,)),
        ],
        compiler_params=pltpu.CompilerParams(vmem_limit_bytes=VMEM_LIMIT),
        cost_estimate=pl.CostEstimate(
            flops=10 * total * width * half,
            bytes_accessed=6 * half * width + 6 * total * width,
            transcendentals=total * half,
        ),
    )(*sources, *pieces, *tables)
    return into, joint[:, 0]


def pick_kernel(table, rows, out):
    out[...] = jnp.dot(table[...], rows[...], preferred_element_type=F32).astype(BF)


def pick_rows(table, source):
    rows, depth = table.shape
    width = source.shape[1]
    block = 512 if width % 512 == 0 else 128
    return pl.pallas_call(
        pick_kernel,
        grid=(width // block,),
        in_specs=[
            pl.BlockSpec((rows, depth), lambda i: (0, 0)),
            pl.BlockSpec((depth, block), lambda i: (0, i)),
        ],
        out_specs=pl.BlockSpec((rows, block), lambda i: (0, i)),
        out_shape=jax.ShapeDtypeStruct((rows, width), BF),
        compiler_params=pltpu.CompilerParams(vmem_limit_bytes=VMEM_LIMIT),
        cost_estimate=pl.CostEstimate(
            flops=2 * rows * depth * width,
            bytes_accessed=2 * width * (rows + depth),
            transcendentals=0,
        ),
    )(table, source)


def slots_of(routes, experts):
    tok = routes.shape[0]
    flat = routes.reshape(2 * tok, 1)
    hits = (flat == lax.broadcasted_iota(jnp.int32, (1, experts), 1)).astype(BF)
    place = lax.broadcasted_iota(jnp.int32, (2 * tok, 2 * tok), 0)
    before = (lax.broadcasted_iota(jnp.int32, (2 * tok, 2 * tok), 1) < place).astype(BF)
    places = jnp.dot(before, hits, preferred_element_type=F32)
    return jnp.sum(hits.astype(F32) * places, -1).astype(jnp.int32).reshape(tok, 2)


def spread(index, rows):
    return index[..., None] == lax.broadcasted_iota(jnp.int32, (1, 1, rows), 2)


def picker(index, rows):
    hits = lax.broadcasted_iota(jnp.int32, (rows, 1), 0)
    return (hits == index[:, 0][None]).astype(BF) + (hits == index[:, 1][None]).astype(BF)


def router_weights(normed, router, chosen):
    logits = jnp.dot(normed.astype(F32), router, precision=HIGHEST)
    picked = jnp.sum(jnp.where(chosen, logits[:, None, :], 0.0), -1)
    one = jax.nn.sigmoid(picked[:, 0:1] - picked[:, 1:2])
    return jnp.concatenate([one, 1.0 - one], 1)


def mix(index, weights, rows, cap):
    count = rows.shape[0]
    tables = []
    for shift in (0, cap):
        hot = spread(index + shift, count)
        tables.append(jnp.sum(jnp.where(hot, weights[..., None], 0.0), 1).astype(BF))
    tok = index.shape[0]
    sides = jnp.dot(jnp.concatenate(tables, 0), rows, preferred_element_type=F32)
    return jnp.concatenate([sides[:tok], sides[tok:]], 1)


def body(
    tokens,
    cotangent,
    norm_gain,
    router,
    dense_gate,
    dense_up,
    dense_down,
    expert_gate,
    expert_up,
    expert_down,
    routes,
):
    tok, width = tokens.shape
    experts = router.shape[1]
    cap = 5 * tok // (2 * experts)
    block = 2 * cap
    everything = experts * block

    values = tokens.astype(F32)
    inverse = lax.rsqrt(jnp.mean(values * values, -1, keepdims=True) + EPS)
    normed = (values * inverse * norm_gain).astype(BF)
    pair = jnp.concatenate([normed, cotangent], 0)

    early = tok // 2
    peer_cot = {k: receive_from(cotangent[:early], k) for k in (1, 3)}
    expert = weight_pieces(expert_gate[0], expert_up[0], expert_down[0])
    far_routes = receive_from(routes, 2)

    def pick_for(rows, index):
        places = jnp.concatenate([index, index + cap], 0)
        return pick_rows(picker(places, everything), rows)

    own_index = routes * block + slots_of(routes, experts)
    far_index = far_routes * block + slots_of(far_routes, experts)
    ready = tuple(peer_cot.values()) + (expert[1], expert[3], far_routes)
    own_send = after(pick_for(pair, own_index), *ready)
    own = over(own_send)
    far_pair = receive_from(pair, 2)
    others = jnp.concatenate([cotangent[early:], normed], 0)
    peer_rest = {k: receive_from(others, k) for k in (1, 3)}
    dense = weight_pieces(*(after(v, own_send) for v in (dense_gate, dense_up, dense_down)))
    chunk = everything // 2
    parts = [own[:chunk], own[chunk:]]
    near = [{k: receive_from(part, k) for k in (1, 3)} for part in parts]
    far = over(pick_for(after(far_pair, *parts), far_index))
    table = shuffle_table(cap, experts // 2)
    tables = (table, table.T)

    own_into, own_joint = hidden_grads([(own,)], expert, tables)
    dense_part, unused = hidden_grads(
        [
            (after(pair, own_into),),
            (peer_cot[1], peer_rest[1]),
            (far_pair,),
            (peer_cot[3], peer_rest[3]),
        ],
        dense,
    )
    far_into, far_joint = hidden_grads([(after(far, dense_part),)], expert, tables)
    far_back = over(far_into)
    near_into = [None, None]
    near_joint = [None, None]
    near_into[0], near_joint[0] = hidden_grads(
        [(after(near[0][1], far_into),), (near[0][3],)], expert, tables
    )
    near_into[1], near_joint[1] = hidden_grads(
        [(after(near[1][1], near_into[0]),), (near[1][3],)], expert, tables
    )
    near_into[1] = after(near_into[1], far_back)
    arrived = (near[1][1], near[1][3])
    home1 = send_to(after(dense_part[tok : 2 * tok], *arrived), 1)
    home3 = send_to(after(dense_part[3 * tok :], *arrived), 3)
    near_back = []
    for i in (0, 1):
        first = after(near_into[i], home1, home3) if i == 0 else near_into[i]
        near_back.append(send_to(first[:chunk], 1).astype(F32) + send_to(first[chunk:], 3).astype(F32))

    joints = jnp.stack(
        [
            own_joint.reshape(experts, cap),
            jnp.concatenate([v[: chunk // 2] for v in near_joint]).reshape(experts, cap),
            far_joint.reshape(experts, cap),
            jnp.concatenate([v[chunk // 2 :] for v in near_joint]).reshape(experts, cap),
        ],
        1,
    )
    joints = over(after(joints.reshape(experts, PEERS * cap), far_back))
    joints = joints.reshape(experts, PEERS, cap)
    shares = [send_to(joints[:, k], k) for k in (1, 2, 3)]

    own_sum = own_into.astype(F32) + jnp.concatenate(near_back, 0)
    own_sum = after(own_sum.astype(BF), joints)
    own_back = over(own_sum)
    score = after(joints[:, 0], own_sum)
    for share in shares:
        score = score + share

    ids = lax.broadcasted_iota(jnp.int32, (1, 1, experts), 2)
    chosen = routes[..., None] == ids
    weights = router_weights(normed, router, chosen)
    far_weights = router_weights(far_pair[:tok], router, far_routes[..., None] == ids)
    mixed = dense_part[2 * tok : 3 * tok].astype(F32)
    mixed = mixed + mix(far_index, far_weights, far_back, cap)
    home2 = send_to(mixed.astype(BF), 2)

    scores = jnp.sum(
        jnp.where(
            spread(routes * cap + own_index - routes * block, experts * cap),
            score.reshape(1, 1, -1),
            0.0,
        ),
        -1,
    )
    delta = weights[:, 0] * weights[:, 1] * (scores[:, 0] - scores[:, 1])
    signed = chosen[:, 0].astype(F32) - chosen[:, 1].astype(F32)
    grad_logits = signed * delta[:, None]
    local_router = lax.dot_general(
        grad_logits, normed.astype(F32), (((0,), (0,)), ((), ())), precision=HIGHEST
    )
    known = dense_part[:tok].astype(F32)
    known = known + jnp.dot(grad_logits, router.T, precision=HIGHEST)
    for piece in (home1, home3):
        known = known + piece.astype(F32)

    total = known + home2.astype(F32) + mix(own_index, weights, own_back, cap)
    local_gain = jnp.sum(total * values * inverse, 0, keepdims=True)
    axes = ("ep", "y", "core")
    devices = lax.axis_size(axes)
    local = jnp.concatenate([local_router, local_gain], 0).reshape(devices, -1)
    mine = jnp.sum(over(local, axes), 0, keepdims=True)
    sums = over(jnp.broadcast_to(mine, local.shape), axes).reshape(experts + 1, width)
    scaled = total * norm_gain
    mean_term = jnp.mean(scaled * values, -1, keepdims=True)
    input_grad = cotangent.astype(F32) + inverse * (
        scaled - values * inverse * inverse * mean_term
    )
    return (input_grad.astype(BF), sums[experts], sums[:experts].T)


def solution(mesh):
    ep, sp = mesh.devices.shape
    grid = Mesh(mesh.devices.reshape(ep, sp // 2, 2), ("ep", "y", "core"))
    shared = ("y", "core")
    rows = ("ep", "y", "core")
    return jax.shard_map(
        body,
        mesh=grid,
        in_specs=(
            P(rows, None),
            P(rows, None),
            P(),
            P(),
            P(None, shared),
            P(None, shared),
            P(shared, None),
            P("ep", None, shared),
            P("ep", None, shared),
            P("ep", shared, None),
            P(rows, None),
        ),
        out_specs=(P(rows, None), P(), P()),
        check_vma=False,
    )
```

```python
import jax
import jax.numpy as jnp
from jax import lax
from jax.experimental import pallas as pl
from jax.experimental.pallas import tpu as pltpu
from jax.sharding import Mesh, PartitionSpec as P

EPS = 1e-05
BF = jnp.bfloat16
F32 = jnp.float32
HIGHEST = lax.Precision.HIGHEST
PEERS = 4
VMEM_LIMIT = 50 * 1024 * 1024
TRANS = (((1,), (1,)), ((), ()))


def receive_from(value, k):
    return lax.ppermute(value, "y", [(i, (i - k) % PEERS) for i in range(PEERS)])


def send_to(value, k):
    return lax.ppermute(value, "y", [(i, (i + k) % PEERS) for i in range(PEERS)])


def swap(value):
    return lax.ppermute(value, "core", [(0, 1), (1, 0)])


def over(value, axes="ep"):
    return lax.all_to_all(value, axes, split_axis=0, concat_axis=0, tiled=True)


def after(value, *others):
    return lax.optimization_barrier((value,) + others)[0]


def weight_pieces(gate, up, down):
    both = [gate.T, up.T, down]
    return [piece for value in both for piece in (value, swap(value))]


def shuffle_table(cap, group):
    size = 2 * group * cap
    row = lax.broadcasted_iota(jnp.int32, (size, size), 0)
    col = lax.broadcasted_iota(jnp.int32, (size, size), 1)
    part, left = row // (group * cap), row % (group * cap)
    return (col == left // cap * (2 * cap) + part * cap + left % cap).astype(BF)


def hidden_kernel(lengths, mixed, *refs):
    count = sum(lengths)
    taken, sources = 0, []
    for length in lengths:
        sources.append(refs[taken : taken + length])
        taken += length
    pieces = refs[count : count + 6]
    refs = refs[count + 6 :]
    if mixed:
        table, table_back = refs[:2]
        refs = refs[2:]
    into, joint, weights, normed, other, both, back, grads, sems = refs
    step = pl.program_id(0)
    part, width = pieces[0].shape
    half = weights.shape[0] // 3
    copies = []
    for i in range(6):
        start = i // 2 * half + i % 2 * part
        copies.append(
            pltpu.make_async_copy(pieces[i], weights.at[pl.ds(start, part), :], sems.at[i])
        )

    @pl.when(step == 0)
    def _():
        for copy in copies[4:] + copies[:4]:
            copy.start()
        if half > 2 * part:
            for i in range(3):
                weights[i * half + 2 * part : (i + 1) * half, :] = jnp.zeros(
                    (half - 2 * part, width), BF
                )

    size = sources[0][0].shape[0] // 2
    each = normed.shape[0] // size
    for p in range(len(lengths)):

        @pl.when(step == p // each)
        def _(p=p):
            first = p % each * size
            if mixed:
                chunk = table.shape[0]
                for i in range(2 * size // chunk):
                    got = jnp.dot(
                        table[...],
                        sources[p][0][i * chunk : (i + 1) * chunk, :],
                        preferred_element_type=F32,
                    ).astype(BF)
                    at = slice(first + i * chunk // 2, first + (i + 1) * chunk // 2)
                    normed[at, :] = got[: chunk // 2]
                    other[at, :] = got[chunk // 2 :]
            else:
                at = slice(first, first + size)
                if lengths[p] == 1:
                    normed[at, :] = sources[p][0][:size, :]
                    other[at, :] = sources[p][0][size:, :]
                else:
                    head, rest = sources[p]
                    early = head.shape[0]
                    late = size - early
                    normed[at, :] = rest[late:, :]
                    other[first : first + early, :] = head[...]
                    other[first + early : first + size, :] = rest[:late, :]

    def wait(i, j):
        @pl.when(step == 0)
        def _():
            for copy in copies[i:j]:
                copy.wait()

    wait(4, 6)
    back[...] = lax.dot_general(
        other[...], weights[2 * half :, :], TRANS, preferred_element_type=F32
    )
    wait(0, 4)
    both[...] = lax.dot_general(
        normed[...], weights[: 2 * half, :], TRANS, preferred_element_type=F32
    )
    gate, up, dy = both[:, :half], both[:, half:], back[...]
    sig = jax.nn.sigmoid(gate)
    active = gate * sig
    grad_up = dy * active
    grads[:, half:] = grad_up.astype(BF)
    grads[:, :half] = (dy * up * (sig + active * (1.0 - sig))).astype(BF)
    score = jnp.sum(grad_up * up, -1, keepdims=True)
    joint[...] = jnp.broadcast_to(score, joint.shape)
    if mixed:
        other[...] = jnp.dot(
            grads[...], weights[: 2 * half, :], preferred_element_type=F32
        ).astype(BF)
        chunk = table.shape[0]
        for i in range(2 * normed.shape[0] // chunk):
            at = slice(i * chunk // 2, (i + 1) * chunk // 2)
            sides = jnp.concatenate([other[at, : width // 2], other[at, width // 2 :]], 0)
            into[i * chunk : (i + 1) * chunk, :] = jnp.dot(
                table_back[...], sides, preferred_element_type=F32
            ).astype(BF)
    else:
        into[...] = jnp.dot(
            grads[...], weights[: 2 * half, :], preferred_element_type=F32
        ).astype(BF)


def hidden_grads(sources, pieces, tables=()):
    count = len(sources)
    lengths = [len(v) for v in sources]
    mixed = len(tables) > 0
    size = sources[0][0].shape[0] // 2
    sources = [v for source in sources for v in source]
    part, width = pieces[0].shape
    half = -(-2 * part // 128) * 128
    total = count * size
    step_rows = min(total, 320) if mixed else 2 * size
    out = (2 * total, width // 2) if mixed else (total, width)
    block = (2 * step_rows, width // 2) if mixed else (step_rows, width)

    def whole(value):
        return pl.BlockSpec(value.shape, lambda i: (0, 0), pipeline_mode=pl.Buffered(1))

    into, joint = pl.pallas_call(
        lambda *refs: hidden_kernel(lengths, mixed, *refs),
        grid=(total // step_rows,),
        in_specs=[whole(v) for v in sources]
        + [pl.BlockSpec(memory_space=pl.ANY)] * 6
        + [whole(v) for v in tables],
        out_specs=[
            pl.BlockSpec(block, lambda i: (i, 0)),
            pl.BlockSpec((step_rows, 128), lambda i: (i, 0)),
        ],
        out_shape=[jax.ShapeDtypeStruct(out, BF), jax.ShapeDtypeStruct((total, 128), F32)],
        scratch_shapes=[
            pltpu.VMEM((3 * half, width), BF),
            pltpu.VMEM((step_rows, width), BF),
            pltpu.VMEM((step_rows, width), BF),
            pltpu.VMEM((step_rows, 2 * half), F32),
            pltpu.VMEM((step_rows, half), F32),
            pltpu.VMEM((step_rows, 2 * half), BF),
            pltpu.SemaphoreType.DMA((6,)),
        ],
        compiler_params=pltpu.CompilerParams(vmem_limit_bytes=VMEM_LIMIT),
        cost_estimate=pl.CostEstimate(
            flops=10 * total * width * half,
            bytes_accessed=6 * half * width + 6 * total * width,
            transcendentals=total * half,
        ),
    )(*sources, *pieces, *tables)
    return into, joint[:, 0]


def pick_kernel(table, rows, out):
    out[...] = jnp.dot(table[...], rows[...], preferred_element_type=F32).astype(BF)


def pick_rows(table, source):
    rows, depth = table.shape
    width = source.shape[1]
    block = 512 if width % 512 == 0 else 128
    return pl.pallas_call(
        pick_kernel,
        grid=(width // block,),
        in_specs=[
            pl.BlockSpec((rows, depth), lambda i: (0, 0)),
            pl.BlockSpec((depth, block), lambda i: (0, i)),
        ],
        out_specs=pl.BlockSpec((rows, block), lambda i: (0, i)),
        out_shape=jax.ShapeDtypeStruct((rows, width), BF),
        compiler_params=pltpu.CompilerParams(vmem_limit_bytes=VMEM_LIMIT),
        cost_estimate=pl.CostEstimate(
            flops=2 * rows * depth * width,
            bytes_accessed=2 * width * (rows + depth),
            transcendentals=0,
        ),
    )(table, source)


def slots_of(routes, experts):
    tok = routes.shape[0]
    flat = routes.reshape(2 * tok, 1)
    hits = (flat == lax.broadcasted_iota(jnp.int32, (1, experts), 1)).astype(BF)
    place = lax.broadcasted_iota(jnp.int32, (2 * tok, 2 * tok), 0)
    before = (lax.broadcasted_iota(jnp.int32, (2 * tok, 2 * tok), 1) < place).astype(BF)
    places = jnp.dot(before, hits, preferred_element_type=F32)
    return jnp.sum(hits.astype(F32) * places, -1).astype(jnp.int32).reshape(tok, 2)


def spread(index, rows):
    return index[..., None] == lax.broadcasted_iota(jnp.int32, (1, 1, rows), 2)


def picker(index, rows):
    hits = lax.broadcasted_iota(jnp.int32, (rows, 1), 0)
    return (hits == index[:, 0][None]).astype(BF) + (hits == index[:, 1][None]).astype(BF)


def router_weights(normed, router, chosen):
    logits = jnp.dot(normed.astype(F32), router, precision=HIGHEST)
    picked = jnp.sum(jnp.where(chosen, logits[:, None, :], 0.0), -1)
    one = jax.nn.sigmoid(picked[:, 0:1] - picked[:, 1:2])
    return jnp.concatenate([one, 1.0 - one], 1)


def mix(index, weights, rows, cap):
    count = rows.shape[0]
    tables = []
    for shift in (0, cap):
        hot = spread(index + shift, count)
        tables.append(jnp.sum(jnp.where(hot, weights[..., None], 0.0), 1).astype(BF))
    tok = index.shape[0]
    sides = jnp.dot(jnp.concatenate(tables, 0), rows, preferred_element_type=F32)
    return jnp.concatenate([sides[:tok], sides[tok:]], 1)


def body(
    tokens,
    cotangent,
    norm_gain,
    router,
    dense_gate,
    dense_up,
    dense_down,
    expert_gate,
    expert_up,
    expert_down,
    routes,
):
    tok, width = tokens.shape
    experts = router.shape[1]
    cap = 5 * tok // (2 * experts)
    block = 2 * cap
    everything = experts * block

    values = tokens.astype(F32)
    inverse = lax.rsqrt(jnp.mean(values * values, -1, keepdims=True) + EPS)
    normed = (values * inverse * norm_gain).astype(BF)
    pair = jnp.concatenate([normed, cotangent], 0)

    early = tok // 2
    peer_cot = {k: receive_from(cotangent[:early], k) for k in (1, 3)}
    expert = weight_pieces(expert_gate[0], expert_up[0], expert_down[0])
    far_routes = receive_from(routes, 2)

    def pick_for(rows, index):
        places = jnp.concatenate([index, index + cap], 0)
        return pick_rows(picker(places, everything), rows)

    own_index = routes * block + slots_of(routes, experts)
    far_index = far_routes * block + slots_of(far_routes, experts)
    ready = tuple(peer_cot.values()) + (expert[1], expert[3], far_routes)
    own_send = after(pick_for(pair, own_index), *ready)
    own = over(own_send)
    far_pair = receive_from(pair, 2)
    others = jnp.concatenate([cotangent[early:], normed], 0)
    peer_rest = {k: receive_from(others, k) for k in (1, 3)}
    dense = weight_pieces(*(after(v, own_send) for v in (dense_gate, dense_up, dense_down)))
    chunk = everything // 2
    parts = [own[:chunk], own[chunk:]]
    near = [{k: receive_from(parts[0], k) for k in (1, 3)}]
    second = after(parts[1], near[0][1], near[0][3])
    near.append({k: receive_from(second, k) for k in (1, 3)})
    far = over(pick_for(after(far_pair, *parts), far_index))
    table = shuffle_table(cap, experts // 2)
    tables = (table, table.T)

    own_into, own_joint = hidden_grads([(own,)], expert, tables)
    dense_part, unused = hidden_grads(
        [
            (after(pair, own_into),),
            (peer_cot[1], peer_rest[1]),
            (far_pair,),
            (peer_cot[3], peer_rest[3]),
        ],
        dense,
    )
    near_into = [None, None]
    near_joint = [None, None]
    near_into[0], near_joint[0] = hidden_grads(
        [(after(near[0][1], dense_part),), (near[0][3],)], expert, tables
    )
    far_into, far_joint = hidden_grads([(after(far, near_into[0]),)], expert, tables)
    far_back = over(far_into)
    near_into[1], near_joint[1] = hidden_grads(
        [(after(near[1][1], far_into),), (near[1][3],)], expert, tables
    )
    first = after(near_into[0], near[1][1], near[1][3])
    first_back = (send_to(first[:chunk], 1), send_to(first[chunk:], 3))
    home1 = send_to(after(dense_part[tok : 2 * tok], *first_back), 1)
    home3 = send_to(after(dense_part[3 * tok :], *first_back), 3)
    other = after(near_into[1], far_back, home1, home3)
    other_back = (send_to(other[:chunk], 1), send_to(other[chunk:], 3))
    near_back = [v[0].astype(F32) + v[1].astype(F32) for v in (first_back, other_back)]

    joints = jnp.stack(
        [
            own_joint.reshape(experts, cap),
            jnp.concatenate([v[: chunk // 2] for v in near_joint]).reshape(experts, cap),
            far_joint.reshape(experts, cap),
            jnp.concatenate([v[chunk // 2 :] for v in near_joint]).reshape(experts, cap),
        ],
        1,
    )
    joints = over(after(joints.reshape(experts, PEERS * cap), far_back))
    joints = joints.reshape(experts, PEERS, cap)
    shares = [send_to(joints[:, k], k) for k in (1, 2, 3)]

    own_sum = own_into.astype(F32) + jnp.concatenate(near_back, 0)
    own_sum = after(own_sum.astype(BF), joints)
    own_back = over(own_sum)
    score = after(joints[:, 0], own_sum)
    for share in shares:
        score = score + share

    ids = lax.broadcasted_iota(jnp.int32, (1, 1, experts), 2)
    chosen = routes[..., None] == ids
    weights = router_weights(normed, router, chosen)
    far_weights = router_weights(far_pair[:tok], router, far_routes[..., None] == ids)
    mixed = dense_part[2 * tok : 3 * tok].astype(F32)
    mixed = mixed + mix(far_index, far_weights, far_back, cap)
    home2 = send_to(mixed.astype(BF), 2)

    scores = jnp.sum(
        jnp.where(
            spread(routes * cap + own_index - routes * block, experts * cap),
            score.reshape(1, 1, -1),
            0.0,
        ),
        -1,
    )
    delta = weights[:, 0] * weights[:, 1] * (scores[:, 0] - scores[:, 1])
    signed = chosen[:, 0].astype(F32) - chosen[:, 1].astype(F32)
    grad_logits = signed * delta[:, None]
    local_router = lax.dot_general(
        grad_logits, normed.astype(F32), (((0,), (0,)), ((), ())), precision=HIGHEST
    )
    known = dense_part[:tok].astype(F32)
    known = known + jnp.dot(grad_logits, router.T, precision=HIGHEST)
    for piece in (home1, home3):
        known = known + piece.astype(F32)

    total = known + home2.astype(F32) + mix(own_index, weights, own_back, cap)
    local_gain = jnp.sum(total * values * inverse, 0, keepdims=True)
    axes = ("ep", "y", "core")
    devices = lax.axis_size(axes)
    local = jnp.concatenate([local_router, local_gain], 0).reshape(devices, -1)
    mine = jnp.sum(over(local, axes), 0, keepdims=True)
    sums = over(jnp.broadcast_to(mine, local.shape), axes).reshape(experts + 1, width)
    scaled = total * norm_gain
    mean_term = jnp.mean(scaled * values, -1, keepdims=True)
    input_grad = cotangent.astype(F32) + inverse * (
        scaled - values * inverse * inverse * mean_term
    )
    return (input_grad.astype(BF), sums[experts], sums[:experts].T)


def solution(mesh):
    ep, sp = mesh.devices.shape
    grid = Mesh(mesh.devices.reshape(ep, sp // 2, 2), ("ep", "y", "core"))
    shared = ("y", "core")
    rows = ("ep", "y", "core")
    return jax.shard_map(
        body,
        mesh=grid,
        in_specs=(
            P(rows, None),
            P(rows, None),
            P(),
            P(),
            P(None, shared),
            P(None, shared),
            P(shared, None),
            P("ep", None, shared),
            P("ep", None, shared),
            P("ep", shared, None),
            P(rows, None),
        ),
        out_specs=(P(rows, None), P(), P()),
        check_vma=False,
    )
```

```python
import jax
import jax.numpy as jnp
from jax import lax
from jax.experimental import pallas as pl
from jax.experimental.pallas import tpu as pltpu
from jax.sharding import Mesh, PartitionSpec as P

EPS = 1e-05
BF = jnp.bfloat16
F32 = jnp.float32
HIGHEST = lax.Precision.HIGHEST
PEERS = 4
VMEM_LIMIT = 50 * 1024 * 1024
TRANS = (((1,), (1,)), ((), ()))


def receive_from(value, k):
    return lax.ppermute(value, "y", [(i, (i - k) % PEERS) for i in range(PEERS)])


def send_to(value, k):
    return lax.ppermute(value, "y", [(i, (i + k) % PEERS) for i in range(PEERS)])


def swap(value):
    return lax.ppermute(value, "core", [(0, 1), (1, 0)])


def over(value, axes="ep"):
    return lax.all_to_all(value, axes, split_axis=0, concat_axis=0, tiled=True)


def after(value, *others):
    return lax.optimization_barrier((value,) + others)[0]


def weight_pieces(gate, up, down):
    both = [gate.T, up.T, down]
    return [piece for value in both for piece in (value, swap(value))]


def shuffle_table(cap, group):
    size = 2 * group * cap
    row = lax.broadcasted_iota(jnp.int32, (size, size), 0)
    col = lax.broadcasted_iota(jnp.int32, (size, size), 1)
    part, left = row // (group * cap), row % (group * cap)
    return (col == left // cap * (2 * cap) + part * cap + left % cap).astype(BF)


def hidden_kernel(lengths, mixed, *refs):
    count = sum(lengths)
    taken, sources = 0, []
    for length in lengths:
        sources.append(refs[taken : taken + length])
        taken += length
    pieces = refs[count : count + 6]
    refs = refs[count + 6 :]
    if mixed:
        table, table_back = refs[:2]
        refs = refs[2:]
    into, joint, weights, normed, other, both, back, grads, sems = refs
    step = pl.program_id(0)
    part, width = pieces[0].shape
    half = weights.shape[0] // 3
    copies = []
    for i in range(6):
        start = i // 2 * half + i % 2 * part
        copies.append(
            pltpu.make_async_copy(pieces[i], weights.at[pl.ds(start, part), :], sems.at[i])
        )

    @pl.when(step == 0)
    def _():
        for copy in copies[4:] + copies[:4]:
            copy.start()
        if half > 2 * part:
            for i in range(3):
                weights[i * half + 2 * part : (i + 1) * half, :] = jnp.zeros(
                    (half - 2 * part, width), BF
                )

    size = sources[0][0].shape[0] // 2
    each = normed.shape[0] // size
    for p in range(len(lengths)):

        @pl.when(step == p // each)
        def _(p=p):
            first = p % each * size
            if mixed:
                chunk = table.shape[0]
                for i in range(2 * size // chunk):
                    got = jnp.dot(
                        table[...],
                        sources[p][0][i * chunk : (i + 1) * chunk, :],
                        preferred_element_type=F32,
                    ).astype(BF)
                    at = slice(first + i * chunk // 2, first + (i + 1) * chunk // 2)
                    normed[at, :] = got[: chunk // 2]
                    other[at, :] = got[chunk // 2 :]
            else:
                at = slice(first, first + size)
                if lengths[p] == 1:
                    normed[at, :] = sources[p][0][:size, :]
                    other[at, :] = sources[p][0][size:, :]
                else:
                    normed[at, :] = sources[p][0][...]
                    other[at, :] = sources[p][1][...]

    def wait(i, j):
        @pl.when(step == 0)
        def _():
            for copy in copies[i:j]:
                copy.wait()

    wait(4, 6)
    back[...] = lax.dot_general(
        other[...], weights[2 * half :, :], TRANS, preferred_element_type=F32
    )
    wait(0, 4)
    both[...] = lax.dot_general(
        normed[...], weights[: 2 * half, :], TRANS, preferred_element_type=F32
    )
    gate, up, dy = both[:, :half], both[:, half:], back[...]
    sig = jax.nn.sigmoid(gate)
    active = gate * sig
    grad_up = dy * active
    grads[:, half:] = grad_up.astype(BF)
    grads[:, :half] = (dy * up * (sig + active * (1.0 - sig))).astype(BF)
    score = jnp.sum(grad_up * up, -1, keepdims=True)
    joint[...] = jnp.broadcast_to(score, joint.shape)
    if mixed:
        other[...] = jnp.dot(
            grads[...], weights[: 2 * half, :], preferred_element_type=F32
        ).astype(BF)
        chunk = table.shape[0]
        for i in range(2 * normed.shape[0] // chunk):
            at = slice(i * chunk // 2, (i + 1) * chunk // 2)
            sides = jnp.concatenate([other[at, : width // 2], other[at, width // 2 :]], 0)
            into[i * chunk : (i + 1) * chunk, :] = jnp.dot(
                table_back[...], sides, preferred_element_type=F32
            ).astype(BF)
    else:
        into[...] = jnp.dot(
            grads[...], weights[: 2 * half, :], preferred_element_type=F32
        ).astype(BF)


def hidden_grads(sources, pieces, tables=()):
    count = len(sources)
    lengths = [len(v) for v in sources]
    mixed = len(tables) > 0
    size = sources[0][0].shape[0] // 2
    sources = [v for source in sources for v in source]
    part, width = pieces[0].shape
    half = -(-2 * part // 128) * 128
    total = count * size
    step_rows = min(total, 320) if mixed else 2 * size
    out = (2 * total, width // 2) if mixed else (total, width)
    block = (2 * step_rows, width // 2) if mixed else (step_rows, width)

    def whole(value):
        return pl.BlockSpec(value.shape, lambda i: (0, 0), pipeline_mode=pl.Buffered(1))

    into, joint = pl.pallas_call(
        lambda *refs: hidden_kernel(lengths, mixed, *refs),
        grid=(total // step_rows,),
        in_specs=[whole(v) for v in sources]
        + [pl.BlockSpec(memory_space=pl.ANY)] * 6
        + [whole(v) for v in tables],
        out_specs=[
            pl.BlockSpec(block, lambda i: (i, 0)),
            pl.BlockSpec((step_rows, 128), lambda i: (i, 0)),
        ],
        out_shape=[jax.ShapeDtypeStruct(out, BF), jax.ShapeDtypeStruct((total, 128), F32)],
        scratch_shapes=[
            pltpu.VMEM((3 * half, width), BF),
            pltpu.VMEM((step_rows, width), BF),
            pltpu.VMEM((step_rows, width), BF),
            pltpu.VMEM((step_rows, 2 * half), F32),
            pltpu.VMEM((step_rows, half), F32),
            pltpu.VMEM((step_rows, 2 * half), BF),
            pltpu.SemaphoreType.DMA((6,)),
        ],
        compiler_params=pltpu.CompilerParams(vmem_limit_bytes=VMEM_LIMIT),
        cost_estimate=pl.CostEstimate(
            flops=10 * total * width * half,
            bytes_accessed=6 * half * width + 6 * total * width,
            transcendentals=total * half,
        ),
    )(*sources, *pieces, *tables)
    return into, joint[:, 0]


def pick_kernel(table, rows, out):
    out[...] = jnp.dot(table[...], rows[...], preferred_element_type=F32).astype(BF)


def pick_rows(table, source):
    rows, depth = table.shape
    width = source.shape[1]
    block = 512 if width % 512 == 0 else 128
    return pl.pallas_call(
        pick_kernel,
        grid=(width // block,),
        in_specs=[
            pl.BlockSpec((rows, depth), lambda i: (0, 0)),
            pl.BlockSpec((depth, block), lambda i: (0, i)),
        ],
        out_specs=pl.BlockSpec((rows, block), lambda i: (0, i)),
        out_shape=jax.ShapeDtypeStruct((rows, width), BF),
        compiler_params=pltpu.CompilerParams(vmem_limit_bytes=VMEM_LIMIT),
        cost_estimate=pl.CostEstimate(
            flops=2 * rows * depth * width,
            bytes_accessed=2 * width * (rows + depth),
            transcendentals=0,
        ),
    )(table, source)


def slots_of(routes, experts):
    tok = routes.shape[0]
    flat = routes.reshape(2 * tok, 1)
    hits = (flat == lax.broadcasted_iota(jnp.int32, (1, experts), 1)).astype(BF)
    place = lax.broadcasted_iota(jnp.int32, (2 * tok, 2 * tok), 0)
    before = (lax.broadcasted_iota(jnp.int32, (2 * tok, 2 * tok), 1) < place).astype(BF)
    places = jnp.dot(before, hits, preferred_element_type=F32)
    return jnp.sum(hits.astype(F32) * places, -1).astype(jnp.int32).reshape(tok, 2)


def spread(index, rows):
    return index[..., None] == lax.broadcasted_iota(jnp.int32, (1, 1, rows), 2)


def picker(index, rows):
    hits = lax.broadcasted_iota(jnp.int32, (rows, 1), 0)
    return (hits == index[:, 0][None]).astype(BF) + (hits == index[:, 1][None]).astype(BF)


def router_weights(normed, router, chosen):
    logits = jnp.dot(normed.astype(F32), router, precision=HIGHEST)
    picked = jnp.sum(jnp.where(chosen, logits[:, None, :], 0.0), -1)
    one = jax.nn.sigmoid(picked[:, 0:1] - picked[:, 1:2])
    return jnp.concatenate([one, 1.0 - one], 1)


def mix(index, weights, rows, cap):
    count = rows.shape[0]
    tables = []
    for shift in (0, cap):
        hot = spread(index + shift, count)
        tables.append(jnp.sum(jnp.where(hot, weights[..., None], 0.0), 1).astype(BF))
    tok = index.shape[0]
    sides = jnp.dot(jnp.concatenate(tables, 0), rows, preferred_element_type=F32)
    return jnp.concatenate([sides[:tok], sides[tok:]], 1)


def body(
    tokens,
    cotangent,
    norm_gain,
    router,
    dense_gate,
    dense_up,
    dense_down,
    expert_gate,
    expert_up,
    expert_down,
    routes,
):
    tok, width = tokens.shape
    experts = router.shape[1]
    cap = 5 * tok // (2 * experts)
    block = 2 * cap
    everything = experts * block

    values = tokens.astype(F32)
    inverse = lax.rsqrt(jnp.mean(values * values, -1, keepdims=True) + EPS)
    normed = (values * inverse * norm_gain).astype(BF)
    pair = jnp.concatenate([normed, cotangent], 0)

    peer_cot = {k: receive_from(cotangent, k) for k in (1, 3)}
    expert = weight_pieces(expert_gate[0], expert_up[0], expert_down[0])
    far_routes = receive_from(routes, 2)

    def pick_for(rows, index):
        places = jnp.concatenate([index, index + cap], 0)
        return pick_rows(picker(places, everything), rows)

    own_index = routes * block + slots_of(routes, experts)
    far_index = far_routes * block + slots_of(far_routes, experts)
    ready = tuple(peer_cot.values()) + tuple(expert[1::2]) + (far_routes,)
    own_send = after(pick_for(pair, own_index), *ready)
    own = over(own_send)
    far_pair = receive_from(pair, 2)
    peer_normed = {k: receive_from(normed, k) for k in (1, 3)}
    dense = weight_pieces(*(after(v, own_send) for v in (dense_gate, dense_up, dense_down)))
    far = over(pick_for(after(far_pair, *dense[1::2]), far_index))
    chunk = everything // 2
    parts = [own[:chunk], own[chunk:]]
    near = [{k: receive_from(part, k) for k in (1, 3)} for part in parts]
    table = shuffle_table(cap, experts // 2)
    tables = (table, table.T)

    own_into, own_joint = hidden_grads([(own,)], expert, tables)
    dense_part, unused = hidden_grads(
        [
            (after(pair, own_into),),
            (peer_normed[1], peer_cot[1]),
            (far_pair,),
            (peer_normed[3], peer_cot[3]),
        ],
        dense,
    )
    far_into, far_joint = hidden_grads([(after(far, dense_part),)], expert, tables)
    far_back = over(far_into)
    near_into = [None, None]
    near_joint = [None, None]
    near_into[0], near_joint[0] = hidden_grads(
        [(after(near[0][1], far_into),), (near[0][3],)], expert, tables
    )
    near_into[1], near_joint[1] = hidden_grads(
        [(after(near[1][1], near_into[0]),), (near[1][3],)], expert, tables
    )
    near_into[1] = after(near_into[1], far_back)
    arrived = (near[1][1], near[1][3])
    near_back = []
    for i in (0, 1):
        first = after(near_into[i], *arrived) if i == 0 else near_into[i]
        near_back.append(send_to(first[:chunk], 1).astype(F32) + send_to(first[chunk:], 3).astype(F32))
    home1 = send_to(after(dense_part[tok : 2 * tok], near_back[1]), 1)
    home3 = send_to(after(dense_part[3 * tok :], near_back[1]), 3)

    joints = jnp.stack(
        [
            own_joint.reshape(experts, cap),
            jnp.concatenate([v[: chunk // 2] for v in near_joint]).reshape(experts, cap),
            far_joint.reshape(experts, cap),
            jnp.concatenate([v[chunk // 2 :] for v in near_joint]).reshape(experts, cap),
        ],
        1,
    )
    joints = over(after(joints.reshape(experts, PEERS * cap), far_back))
    joints = joints.reshape(experts, PEERS, cap)
    shares = [send_to(joints[:, k], k) for k in (1, 2, 3)]

    own_sum = own_into.astype(F32) + jnp.concatenate(near_back, 0)
    own_sum = after(own_sum.astype(BF), joints)
    own_back = over(own_sum)
    score = after(joints[:, 0], own_sum)
    for share in shares:
        score = score + share

    ids = lax.broadcasted_iota(jnp.int32, (1, 1, experts), 2)
    chosen = routes[..., None] == ids
    weights = router_weights(normed, router, chosen)
    far_weights = router_weights(far_pair[:tok], router, far_routes[..., None] == ids)
    mixed = dense_part[2 * tok : 3 * tok].astype(F32)
    mixed = mixed + mix(far_index, far_weights, far_back, cap)
    mixed = mixed.astype(BF)
    home2 = send_to(mixed, 2)
    away = jnp.sum(mixed.astype(F32) * far_pair[:tok].astype(F32), 0)
    for k in (1, 3):
        part = dense_part[k * tok : (k + 1) * tok].astype(F32)
        away = away + jnp.sum(part * peer_normed[k].astype(F32), 0)
    away = away / norm_gain

    scores = jnp.sum(
        jnp.where(
            spread(routes * cap + own_index - routes * block, experts * cap),
            score.reshape(1, 1, -1),
            0.0,
        ),
        -1,
    )
    delta = weights[:, 0] * weights[:, 1] * (scores[:, 0] - scores[:, 1])
    signed = chosen[:, 0].astype(F32) - chosen[:, 1].astype(F32)
    grad_logits = signed * delta[:, None]
    local_router = lax.dot_general(
        grad_logits, normed.astype(F32), (((0,), (0,)), ((), ())), precision=HIGHEST
    )
    early = dense_part[:tok].astype(F32)
    early = early + jnp.dot(grad_logits, router.T, precision=HIGHEST)
    early = early + mix(own_index, weights, own_back, cap)
    local_gain = (jnp.sum(early * values * inverse, 0) + away)[None]
    total = early
    for piece in (home1, home3, home2):
        total = total + piece.astype(F32)
    axes = ("ep", "y", "core")
    devices = lax.axis_size(axes)
    local = jnp.concatenate([local_router, local_gain], 0).reshape(devices, -1)
    mine = jnp.sum(over(local, axes), 0, keepdims=True)
    sums = over(jnp.broadcast_to(mine, local.shape), axes).reshape(experts + 1, width)
    scaled = total * norm_gain
    mean_term = jnp.mean(scaled * values, -1, keepdims=True)
    input_grad = cotangent.astype(F32) + inverse * (
        scaled - values * inverse * inverse * mean_term
    )
    return (input_grad.astype(BF), sums[experts], sums[:experts].T)


def solution(mesh):
    ep, sp = mesh.devices.shape
    grid = Mesh(mesh.devices.reshape(ep, sp // 2, 2), ("ep", "y", "core"))
    shared = ("y", "core")
    rows = ("ep", "y", "core")
    return jax.shard_map(
        body,
        mesh=grid,
        in_specs=(
            P(rows, None),
            P(rows, None),
            P(),
            P(),
            P(None, shared),
            P(None, shared),
            P(shared, None),
            P("ep", None, shared),
            P("ep", None, shared),
            P("ep", shared, None),
            P(rows, None),
        ),
        out_specs=(P(rows, None), P(), P()),
        check_vma=False,
    )
```

```python
import jax
import jax.numpy as jnp
from jax import lax
from jax.experimental import pallas as pl
from jax.experimental.pallas import tpu as pltpu
from jax.sharding import Mesh, PartitionSpec as P

EPS = 1e-05
BF = jnp.bfloat16
F32 = jnp.float32
HIGHEST = lax.Precision.HIGHEST
PEERS = 4
VMEM_LIMIT = 50 * 1024 * 1024
TRANS = (((1,), (1,)), ((), ()))


def receive_from(value, k):
    return lax.ppermute(value, "y", [(i, (i - k) % PEERS) for i in range(PEERS)])


def send_to(value, k):
    return lax.ppermute(value, "y", [(i, (i + k) % PEERS) for i in range(PEERS)])


def swap(value):
    return lax.ppermute(value, "core", [(0, 1), (1, 0)])


def over(value, axes="ep"):
    return lax.all_to_all(value, axes, split_axis=0, concat_axis=0, tiled=True)


def after(value, *others):
    return lax.optimization_barrier((value,) + others)[0]


def weight_pieces(gate, up, down):
    both = [gate.T, up.T, down]
    return [piece for value in both for piece in (value, swap(value))]


def shuffle_table(cap, group):
    size = 2 * group * cap
    row = lax.broadcasted_iota(jnp.int32, (size, size), 0)
    col = lax.broadcasted_iota(jnp.int32, (size, size), 1)
    part, left = row // (group * cap), row % (group * cap)
    return (col == left // cap * (2 * cap) + part * cap + left % cap).astype(BF)


def hidden_kernel(lengths, mixed, *refs):
    count = sum(lengths)
    taken, sources = 0, []
    for length in lengths:
        sources.append(refs[taken : taken + length])
        taken += length
    pieces = refs[count : count + 6]
    refs = refs[count + 6 :]
    if mixed:
        table, table_back = refs[:2]
        refs = refs[2:]
    into, joint, weights, normed, other, both, back, grads, sems = refs
    step = pl.program_id(0)
    part, width = pieces[0].shape
    half = weights.shape[0] // 3
    copies = []
    for i in range(6):
        start = i // 2 * half + i % 2 * part
        copies.append(
            pltpu.make_async_copy(pieces[i], weights.at[pl.ds(start, part), :], sems.at[i])
        )

    @pl.when(step == 0)
    def _():
        for copy in copies[4:] + copies[:4]:
            copy.start()
        if half > 2 * part:
            for i in range(3):
                weights[i * half + 2 * part : (i + 1) * half, :] = jnp.zeros(
                    (half - 2 * part, width), BF
                )

    size = sources[0][0].shape[0] // 2
    each = normed.shape[0] // size
    for p in range(len(lengths)):

        @pl.when(step == p // each)
        def _(p=p):
            first = p % each * size
            if mixed:
                chunk = table.shape[0]
                for i in range(2 * size // chunk):
                    got = jnp.dot(
                        table[...],
                        sources[p][0][i * chunk : (i + 1) * chunk, :],
                        preferred_element_type=F32,
                    ).astype(BF)
                    at = slice(first + i * chunk // 2, first + (i + 1) * chunk // 2)
                    normed[at, :] = got[: chunk // 2]
                    other[at, :] = got[chunk // 2 :]
            else:
                at = slice(first, first + size)
                if lengths[p] == 1:
                    normed[at, :] = sources[p][0][:size, :]
                    other[at, :] = sources[p][0][size:, :]
                else:
                    normed[at, :] = sources[p][0][...]
                    other[at, :] = sources[p][1][...]

    def wait(i, j):
        @pl.when(step == 0)
        def _():
            for copy in copies[i:j]:
                copy.wait()

    wait(4, 6)
    back[...] = lax.dot_general(
        other[...], weights[2 * half :, :], TRANS, preferred_element_type=F32
    )
    wait(0, 4)
    both[...] = lax.dot_general(
        normed[...], weights[: 2 * half, :], TRANS, preferred_element_type=F32
    )
    gate, up, dy = both[:, :half], both[:, half:], back[...]
    sig = jax.nn.sigmoid(gate)
    active = gate * sig
    grad_up = dy * active
    grads[:, half:] = grad_up.astype(BF)
    grads[:, :half] = (dy * up * (sig + active * (1.0 - sig))).astype(BF)
    score = jnp.sum(grad_up * up, -1, keepdims=True)
    joint[...] = jnp.broadcast_to(score, joint.shape)
    if mixed:
        other[...] = jnp.dot(
            grads[...], weights[: 2 * half, :], preferred_element_type=F32
        ).astype(BF)
        chunk = table.shape[0]
        for i in range(2 * normed.shape[0] // chunk):
            at = slice(i * chunk // 2, (i + 1) * chunk // 2)
            sides = jnp.concatenate([other[at, : width // 2], other[at, width // 2 :]], 0)
            into[i * chunk : (i + 1) * chunk, :] = jnp.dot(
                table_back[...], sides, preferred_element_type=F32
            ).astype(BF)
    else:
        into[...] = jnp.dot(
            grads[...], weights[: 2 * half, :], preferred_element_type=F32
        ).astype(BF)


def hidden_grads(sources, pieces, tables=()):
    count = len(sources)
    lengths = [len(v) for v in sources]
    mixed = len(tables) > 0
    size = sources[0][0].shape[0] // 2
    sources = [v for source in sources for v in source]
    part, width = pieces[0].shape
    half = -(-2 * part // 128) * 128
    total = count * size
    step_rows = min(total, 320) if mixed else 2 * size
    out = (2 * total, width // 2) if mixed else (total, width)
    block = (2 * step_rows, width // 2) if mixed else (step_rows, width)

    def whole(value):
        return pl.BlockSpec(value.shape, lambda i: (0, 0), pipeline_mode=pl.Buffered(1))

    into, joint = pl.pallas_call(
        lambda *refs: hidden_kernel(lengths, mixed, *refs),
        grid=(total // step_rows,),
        in_specs=[whole(v) for v in sources]
        + [pl.BlockSpec(memory_space=pl.ANY)] * 6
        + [whole(v) for v in tables],
        out_specs=[
            pl.BlockSpec(block, lambda i: (i, 0)),
            pl.BlockSpec((step_rows, 128), lambda i: (i, 0)),
        ],
        out_shape=[jax.ShapeDtypeStruct(out, BF), jax.ShapeDtypeStruct((total, 128), F32)],
        scratch_shapes=[
            pltpu.VMEM((3 * half, width), BF),
            pltpu.VMEM((step_rows, width), BF),
            pltpu.VMEM((step_rows, width), BF),
            pltpu.VMEM((step_rows, 2 * half), F32),
            pltpu.VMEM((step_rows, half), F32),
            pltpu.VMEM((step_rows, 2 * half), BF),
            pltpu.SemaphoreType.DMA((6,)),
        ],
        compiler_params=pltpu.CompilerParams(vmem_limit_bytes=VMEM_LIMIT),
        cost_estimate=pl.CostEstimate(
            flops=10 * total * width * half,
            bytes_accessed=6 * half * width + 6 * total * width,
            transcendentals=total * half,
        ),
    )(*sources, *pieces, *tables)
    return into, joint[:, 0]


def pick_kernel(table, rows, out):
    out[...] = jnp.dot(table[...], rows[...], preferred_element_type=F32).astype(BF)


def pick_rows(table, source):
    rows, depth = table.shape
    width = source.shape[1]
    block = 512 if width % 512 == 0 else 128
    return pl.pallas_call(
        pick_kernel,
        grid=(width // block,),
        in_specs=[
            pl.BlockSpec((rows, depth), lambda i: (0, 0)),
            pl.BlockSpec((depth, block), lambda i: (0, i)),
        ],
        out_specs=pl.BlockSpec((rows, block), lambda i: (0, i)),
        out_shape=jax.ShapeDtypeStruct((rows, width), BF),
        compiler_params=pltpu.CompilerParams(vmem_limit_bytes=VMEM_LIMIT),
        cost_estimate=pl.CostEstimate(
            flops=2 * rows * depth * width,
            bytes_accessed=2 * width * (rows + depth),
            transcendentals=0,
        ),
    )(table, source)


def slots_of(routes, experts):
    tok = routes.shape[0]
    flat = routes.reshape(2 * tok, 1)
    hits = (flat == lax.broadcasted_iota(jnp.int32, (1, experts), 1)).astype(BF)
    place = lax.broadcasted_iota(jnp.int32, (2 * tok, 2 * tok), 0)
    before = (lax.broadcasted_iota(jnp.int32, (2 * tok, 2 * tok), 1) < place).astype(BF)
    places = jnp.dot(before, hits, preferred_element_type=F32)
    return jnp.sum(hits.astype(F32) * places, -1).astype(jnp.int32).reshape(tok, 2)


def spread(index, rows):
    return index[..., None] == lax.broadcasted_iota(jnp.int32, (1, 1, rows), 2)


def picker(index, rows):
    hits = lax.broadcasted_iota(jnp.int32, (rows, 1), 0)
    return (hits == index[:, 0][None]).astype(BF) + (hits == index[:, 1][None]).astype(BF)


def router_weights(normed, router, chosen):
    logits = jnp.dot(normed.astype(F32), router, precision=HIGHEST)
    picked = jnp.sum(jnp.where(chosen, logits[:, None, :], 0.0), -1)
    one = jax.nn.sigmoid(picked[:, 0:1] - picked[:, 1:2])
    return jnp.concatenate([one, 1.0 - one], 1)


def mix(index, weights, rows, cap):
    count = rows.shape[0]
    tables = []
    for shift in (0, cap):
        hot = spread(index + shift, count)
        tables.append(jnp.sum(jnp.where(hot, weights[..., None], 0.0), 1).astype(BF))
    tok = index.shape[0]
    sides = jnp.dot(jnp.concatenate(tables, 0), rows, preferred_element_type=F32)
    return jnp.concatenate([sides[:tok], sides[tok:]], 1)


def body(
    tokens,
    cotangent,
    norm_gain,
    router,
    dense_gate,
    dense_up,
    dense_down,
    expert_gate,
    expert_up,
    expert_down,
    routes,
):
    tok, width = tokens.shape
    experts = router.shape[1]
    cap = 5 * tok // (2 * experts)
    block = 2 * cap
    everything = experts * block

    values = tokens.astype(F32)
    inverse = lax.rsqrt(jnp.mean(values * values, -1, keepdims=True) + EPS)
    normed = (values * inverse * norm_gain).astype(BF)
    pair = jnp.concatenate([normed, cotangent], 0)

    peer_cot = {k: receive_from(cotangent, k) for k in (1, 3)}
    expert = weight_pieces(expert_gate[0], expert_up[0], expert_down[0])
    far_routes = receive_from(routes, 2)

    def pick_for(rows, index):
        places = jnp.concatenate([index, index + cap], 0)
        return pick_rows(picker(places, everything), rows)

    own_index = routes * block + slots_of(routes, experts)
    far_index = far_routes * block + slots_of(far_routes, experts)
    ready = tuple(peer_cot.values()) + tuple(expert[1::2]) + (far_routes,)
    own_send = after(pick_for(pair, own_index), *ready)
    own = over(own_send)
    far_pair = receive_from(pair, 2)
    peer_normed = {k: receive_from(normed, k) for k in (1, 3)}
    dense = weight_pieces(*(after(v, own_send) for v in (dense_gate, dense_up, dense_down)))
    far = over(pick_for(after(far_pair, *dense[1::2]), far_index))
    chunk = everything // 2
    parts = [own[:chunk], own[chunk:]]
    near = [{k: receive_from(part, k) for k in (1, 3)} for part in parts]
    table = shuffle_table(cap, experts // 2)
    tables = (table, table.T)

    own_into, own_joint = hidden_grads([(own,)], expert, tables)
    dense_part, unused = hidden_grads(
        [
            (after(pair, own_into),),
            (peer_normed[1], peer_cot[1]),
            (far_pair,),
            (peer_normed[3], peer_cot[3]),
        ],
        dense,
    )
    far_into, far_joint = hidden_grads([(after(far, dense_part),)], expert, tables)
    far_back = over(far_into)
    near_into = [None, None]
    near_joint = [None, None]
    near_into[0], near_joint[0] = hidden_grads(
        [(after(near[0][1], far_into),), (near[0][3],)], expert, tables
    )
    near_into[1], near_joint[1] = hidden_grads(
        [(after(near[1][1], near_into[0]),), (near[1][3],)], expert, tables
    )
    near_into[1] = after(near_into[1], far_back)
    arrived = (near[1][1], near[1][3])
    near_back = []
    for i in (0, 1):
        first = after(near_into[i], *arrived) if i == 0 else near_into[i]
        near_back.append(send_to(first[:chunk], 1).astype(F32) + send_to(first[chunk:], 3).astype(F32))
    home1 = send_to(after(dense_part[tok : 2 * tok], near_back[1]), 1)
    home3 = send_to(after(dense_part[3 * tok :], near_back[1]), 3)

    joints = jnp.stack(
        [
            own_joint.reshape(experts, cap),
            jnp.concatenate([v[: chunk // 2] for v in near_joint]).reshape(experts, cap),
            far_joint.reshape(experts, cap),
            jnp.concatenate([v[chunk // 2 :] for v in near_joint]).reshape(experts, cap),
        ],
        1,
    )
    joints = over(after(joints.reshape(experts, PEERS * cap), far_back))
    joints = joints.reshape(experts, PEERS, cap)
    shares = [send_to(joints[:, k], k) for k in (1, 2, 3)]

    own_sum = own_into.astype(F32) + jnp.concatenate(near_back, 0)
    own_sum = after(own_sum.astype(BF), joints)
    own_back = over(own_sum)
    score = after(joints[:, 0], own_sum)
    for share in shares:
        score = score + share

    ids = lax.broadcasted_iota(jnp.int32, (1, 1, experts), 2)
    chosen = routes[..., None] == ids
    weights = router_weights(normed, router, chosen)
    far_weights = router_weights(far_pair[:tok], router, far_routes[..., None] == ids)
    mixed = dense_part[2 * tok : 3 * tok].astype(F32)
    mixed = mixed + mix(far_index, far_weights, far_back, cap)
    mixed = mixed.astype(BF)
    home2 = send_to(mixed, 2)
    away = jnp.sum(mixed.astype(F32) * far_pair[:tok].astype(F32), 0)
    for k in (1, 3):
        part = dense_part[k * tok : (k + 1) * tok].astype(F32)
        away = away + jnp.sum(part * peer_normed[k].astype(F32), 0)
    away = away / norm_gain

    scores = jnp.sum(
        jnp.where(
            spread(routes * cap + own_index - routes * block, experts * cap),
            score.reshape(1, 1, -1),
            0.0,
        ),
        -1,
    )
    delta = weights[:, 0] * weights[:, 1] * (scores[:, 0] - scores[:, 1])
    signed = chosen[:, 0].astype(F32) - chosen[:, 1].astype(F32)
    grad_logits = signed * delta[:, None]
    local_router = lax.dot_general(
        grad_logits, normed.astype(F32), (((0,), (0,)), ((), ())), precision=HIGHEST
    )
    early = dense_part[:tok].astype(F32)
    early = early + jnp.dot(grad_logits, router.T, precision=HIGHEST)
    early = early + mix(own_index, weights, own_back, cap)
    local_gain = (jnp.sum(early * values * inverse, 0) + away)[None]
    axes = ("ep", "y", "core")
    devices = lax.axis_size(axes)
    local = jnp.concatenate([local_router, local_gain], 0).reshape(devices, -1)
    mine = jnp.sum(over(local, axes), 0, keepdims=True)
    total = early
    for piece in lax.optimization_barrier((home1, home3, home2, mine))[:3]:
        total = total + piece.astype(F32)
    sums = over(jnp.broadcast_to(mine, local.shape), axes).reshape(experts + 1, width)
    scaled = total * norm_gain
    mean_term = jnp.mean(scaled * values, -1, keepdims=True)
    input_grad = cotangent.astype(F32) + inverse * (
        scaled - values * inverse * inverse * mean_term
    )
    return (input_grad.astype(BF), sums[experts], sums[:experts].T)


def solution(mesh):
    ep, sp = mesh.devices.shape
    grid = Mesh(mesh.devices.reshape(ep, sp // 2, 2), ("ep", "y", "core"))
    shared = ("y", "core")
    rows = ("ep", "y", "core")
    return jax.shard_map(
        body,
        mesh=grid,
        in_specs=(
            P(rows, None),
            P(rows, None),
            P(),
            P(),
            P(None, shared),
            P(None, shared),
            P(shared, None),
            P("ep", None, shared),
            P("ep", None, shared),
            P("ep", shared, None),
            P(rows, None),
        ),
        out_specs=(P(rows, None), P(), P()),
        check_vma=False,
    )
```
